32 devices in a mesh: fsdp: 4 (over x, core), ctx: 8 (over z, y).
Axes of the slice: x: 2, y: 2, z: 4, core: 2. Of those that a mesh axis runs over, the one named last changes fastest.
Arguments:
- prompt_in: bfloat16 [4, 1024, 1024], P('fsdp', 'ctx'), may hold values from -16 to 16
- cont_in: bfloat16 [4, 8, 512, 1024], P('fsdp', 'ctx'), may hold values from -16 to 16
- encoder: bfloat16 [4, 512, 1024], P('fsdp', 'ctx'), may hold values from -6 to 6
- prompt_start: int32 [4], P('fsdp'), may hold values from 0 to 64, as said below
- cont_start: int32 [4, 8], P('fsdp'), may hold values from 0 to 384, as said below
- self_proj: bfloat16 [1024, 3072], P(('fsdp', 'ctx')), may hold values from -0.1875 to 0.1875
- self_out: bfloat16 [1024, 1024], P(('fsdp', 'ctx')), may hold values from -1.5 to 1.5
- cross_query: bfloat16 [1024, 1024], P(('fsdp', 'ctx')), may hold values from -0.1875 to 0.1875
- cross_kv: bfloat16 [1024, 2048], P(('fsdp', 'ctx')), may hold values from -0.1875 to 0.1875
- cross_out: bfloat16 [1024, 1024], P(('fsdp', 'ctx')), may hold values from -1.5 to 1.5
- up_proj: bfloat16 [1024, 4096], P(('fsdp', 'ctx')), may hold values from -0.1875 to 0.1875
- down_proj: bfloat16 [4096, 1024], P(('fsdp', 'ctx')), may hold values from -0.09375 to 0.09375
- vec_bias: bfloat16 [7, 1024], P(None, ('fsdp', 'ctx')), may hold values from -3 to 3
- up_bias: bfloat16 [4096], P(('fsdp', 'ctx')), may hold values from -3 to 3
- ln_gain: bfloat16 [3, 1024], P(None, ('fsdp', 'ctx')), may hold values from 0.5 to 1.5
- ln_bias: bfloat16 [3, 1024], P(None, ('fsdp', 'ctx')), may hold values from -2 to 2
- prompt_cot: bfloat16 [4, 1024, 1024], P('fsdp', 'ctx'), may hold values from -6 to 6
- cont_cot: bfloat16 [4, 8, 512, 1024], P('fsdp', 'ctx'), may hold values from -6 to 6
Outputs:
- prompt_out: bfloat16 [4, 1024, 1024], P('fsdp', 'ctx')
- cont_out: bfloat16 [4, 8, 512, 1024], P('fsdp', 'ctx')
- prompt_grad: float32 [4, 1024, 1024], P('fsdp', 'ctx')
- cont_grad: float32 [4, 8, 512, 1024], P('fsdp', 'ctx')
- encoder_grad: float32 [4, 512, 1024], P('fsdp', 'ctx')
- self_proj_grad: float32 [1024, 3072], P(('fsdp', 'ctx'))
- self_out_grad: float32 [1024, 1024], P(('fsdp', 'ctx'))
- cross_query_grad: float32 [1024, 1024], P(('fsdp', 'ctx'))
- cross_kv_grad: float32 [1024, 2048], P(('fsdp', 'ctx'))
- cross_out_grad: float32 [1024, 1024], P(('fsdp', 'ctx'))
- up_proj_grad: float32 [1024, 4096], P(('fsdp', 'ctx'))
- down_proj_grad: float32 [4096, 1024], P(('fsdp', 'ctx'))
- vec_bias_grad: float32 [7, 1024], P(None, ('fsdp', 'ctx'))
- up_bias_grad: float32 [4096], P(('fsdp', 'ctx'))
- ln_gain_grad: float32 [3, 1024], P(None, ('fsdp', 'ctx'))
- ln_bias_grad: float32 [3, 1024], P(None, ('fsdp', 'ctx'))
- statistics: float32 [4, 6], P('fsdp')
The draws below stay inside these ranges and needn't reach their ends.
Inputs may be any that keep to these rules, and one draw needn't show every extreme that they name: Prompt positions of a group before its prompt_start are left padding. Some group starts at 0 and some at 64. Places of a continuation slot before its cont_start are left padding; its tokens run to place 512 - 1. Some slot starts at 0 and some at 384.
All inputs are finite; a program needn't handle non-finite values.
Results may differ from the reference program's by a relative error of at most 0.024.
The reference program's roundings to bfloat16 on the way count: a program that leaves them out, or rounds other values in their place, can miss the bound.
Values may be sent and summed in bfloat16 or wider, within the bound.
No kernel may reach another device: no remote copies, remote signals or barrier semaphores. Data moves between devices by JAX's collectives and lax.ppermute only.
A program may use at most 320 MiB of HBM per device.

```python
import jax
import jax.numpy as jnp
from jax import lax

D = 1024
HEADS = 16
HDIM = 64
FF = 4096
PDEV = 128
CDEV = 1
CLEN = 512
GROUPS = 4
PROMPT = 1024
NCONT = 8
ENC = 512
N_CTX = 8


def draw_prompt_start(key, part):
    key = jax.random.fold_in(key, 17)
    first_key, second_key = jax.random.split(key)
    starts = jax.random.randint(first_key, (GROUPS,), 0, PDEV // 2 + 1)
    ordering = jax.random.permutation(second_key, GROUPS)
    starts = starts.at[ordering[0]].set(0)
    starts = starts.at[ordering[1]].set(PDEV // 2)
    return starts.astype(jnp.int32)


def draw_cont_start(key, part):
    key = jax.random.fold_in(key, 29)
    first_key, second_key = jax.random.split(key)
    latest = 3 * CLEN // 4
    starts = jax.random.randint(first_key, (GROUPS * NCONT,), 0, latest + 1)
    ordering = jax.random.permutation(second_key, GROUPS * NCONT)
    starts = starts.at[ordering[0]].set(0)
    starts = starts.at[ordering[1]].set(latest)
    return starts.reshape(GROUPS, NCONT).astype(jnp.int32)


def entries(key, shape):
    return jnp.clip(jax.random.normal(key, shape, jnp.float32), -5.0, 5.0)


def draw_prompt_in(key, part):
    key = jax.random.fold_in(key, 41)
    ramp = 1.0 + 2.0 * jnp.arange(PROMPT, dtype=jnp.float32) / (PROMPT - 1)
    values = entries(key, (GROUPS, PROMPT, D)) * ramp[None, :, None]
    return values.astype(jnp.bfloat16)


def draw_cont_in(key, part):
    key = jax.random.fold_in(key, 53)
    ramp = 1.0 + 2.0 * jnp.arange(NCONT, dtype=jnp.float32) / (NCONT - 1)
    values = entries(key, (GROUPS, NCONT, CLEN, D)) * ramp[None, :, None, None]
    return values.astype(jnp.bfloat16)


def level_of(key, dims, shards, low, high):
    loudness = 1.0
    for dim, shards_of in shards:
        heights = jax.random.uniform(jax.random.fold_in(jax.random.fold_in(key, 6), dim), (shards_of,), jnp.float32, low / len(shards), high / len(shards))
        loudness = loudness * jnp.repeat(jnp.exp(heights), dims[dim] // shards_of).reshape((-1,) + (1,) * (len(dims) - 1 - dim))
    return loudness


def bell_draw(rng, dims, width, most, cuts=(), held_as=jnp.bfloat16):
    drawn = width * jax.random.normal(rng, dims, jnp.float32)
    if cuts:
        drawn = drawn * level_of(rng, dims, cuts, -0.22, 0.18)
    return jnp.clip(drawn, -most, most).astype(held_as)


def setup_inputs(seed: int = 0) -> dict:
    seeds = jax.random.split(jax.random.key(seed), 19)
    prompt_in = draw_prompt_in(jax.random.fold_in(seeds[18], 71), 0)
    cont_in = draw_cont_in(jax.random.fold_in(seeds[18], 71), 0)
    encoder = bell_draw(seeds[2], (GROUPS, ENC, D), 1.0, 6.0, ((0, 4), (1, 8)))
    prompt_start = draw_prompt_start(jax.random.fold_in(seeds[18], 71), 0)
    cont_start = draw_cont_start(jax.random.fold_in(seeds[18], 71), 0)
    self_proj = bell_draw(seeds[5], (D, 3 * D), D ** -0.5, 0.1875, ((0, 32),))
    self_out = bell_draw(seeds[6], (D, D), (D // 64) ** -0.5, 1.5, ((0, 32),))
    cross_query = bell_draw(seeds[7], (D, D), D ** -0.5, 0.1875, ((0, 32),))
    cross_kv = bell_draw(seeds[8], (D, 2 * D), D ** -0.5, 0.1875, ((0, 32),))
    cross_out = bell_draw(seeds[9], (D, D), (D // 64) ** -0.5, 1.5, ((0, 32),))
    up_proj = bell_draw(seeds[10], (D, FF), D ** -0.5, 0.1875, ((0, 32),))
    down_proj = bell_draw(seeds[11], (FF, D), FF ** -0.5, 0.09375, ((0, 32),))
    vec_bias = bell_draw(seeds[12], (7, D), 0.5, 3.0, ((1, 32),))
    up_bias = bell_draw(seeds[13], (FF,), 0.5, 3.0, ((0, 32),))
    ln_gain = jnp.clip(1.0 + 0.1 * jax.random.normal(seeds[14], (3, D), jnp.float32), 0.5, 1.5).astype(jnp.bfloat16)
    ln_bias = bell_draw(seeds[15], (3, D), 0.3, 2.0, ((1, 32),))
    prompt_cot = bell_draw(seeds[16], (GROUPS, PROMPT, D), 1.0, 6.0, ((0, 4), (1, 8)))
    cont_cot = bell_draw(seeds[17], (GROUPS, NCONT, CLEN, D), 1.0, 6.0, ((0, 4), (1, 8)))
    return dict(prompt_in=prompt_in, cont_in=cont_in, encoder=encoder, prompt_start=prompt_start, cont_start=cont_start, self_proj=self_proj, self_out=self_out, cross_query=cross_query, cross_kv=cross_kv, cross_out=cross_out, up_proj=up_proj, down_proj=down_proj, vec_bias=vec_bias, up_bias=up_bias, ln_gain=ln_gain, ln_bias=ln_bias, prompt_cot=prompt_cot, cont_cot=cont_cot)


@jax.custom_vjp
def low(v):
    return lax.optimization_barrier(v.astype(jnp.bfloat16)).astype(jnp.float32)

@jax.custom_vjp
def low_back(v):
    return v

def low_keep(v):
    return (low(v), None)

def low_pass(kept, grad):
    return (grad,)

def back_keep(v):
    return (v, None)

def back_low(kept, grad):
    return (low(grad),)
low.defvjp(low_keep, low_pass)
low_back.defvjp(back_keep, back_low)

def round_both(value):
    return low_back(low(value))

def matmul(first_mat, second_mat):
    return jnp.dot(first_mat, second_mat, precision=lax.Precision.HIGHEST, preferred_element_type=jnp.float32)

def layer_norm(residual, gain_vec, shift_vec):
    row_mean = lax.optimization_barrier(jnp.mean(residual, -1, keepdims=True))
    centred = residual - row_mean
    row_var = lax.optimization_barrier(jnp.mean(centred * centred, -1, keepdims=True))
    return centred * lax.rsqrt(row_var + 1e-05) * gain_vec + shift_vec

def block_mask(block_index, prompt_begin, cont_begin, prompt_rows, ctx_count, slot_count, slot_len):
    prompt_len = prompt_rows * ctx_count
    positions = block_index * prompt_rows + jnp.arange(prompt_rows, dtype=jnp.int32)
    key_spots = jnp.arange(prompt_len, dtype=jnp.int32)
    prompt_part = (key_spots[None, :] <= positions[:, None]) & ((key_spots[None, :] >= prompt_begin) | (key_spots[None, :] == positions[:, None]))
    prompt_part = jnp.concatenate([prompt_part, jnp.zeros((prompt_rows, slot_count * slot_len), bool)], 1)
    slot_index = jnp.arange(slot_count * slot_len, dtype=jnp.int32) // slot_len
    offset_in = jnp.arange(slot_count * slot_len, dtype=jnp.int32) % slot_len
    begin_at = lax.optimization_barrier(jnp.sum(jnp.where(slot_index[:, None] == jnp.arange(slot_count, dtype=jnp.int32)[None, :], cont_begin[None, :], 0), 1))
    prompt_seen = jnp.broadcast_to((key_spots >= prompt_begin)[None, :], (slot_count * slot_len, prompt_len))
    own_keys = (slot_index[:, None] == slot_index[None, :]) & (offset_in[None, :] <= offset_in[:, None]) & ((offset_in[None, :] >= begin_at[:, None]) | (offset_in[None, :] == offset_in[:, None]))
    cont_part = jnp.concatenate([prompt_seen, own_keys], 1)
    return jnp.concatenate([prompt_part, cont_part], 0)

def attend(queries, key_rows, value_rows, allowed):
    row_total = queries.shape[0]
    key_total = key_rows.shape[0]
    head_query = queries.reshape(row_total, HEADS, HDIM)
    head_key = key_rows.reshape(key_total, HEADS, HDIM)
    head_value = value_rows.reshape(key_total, HEADS, HDIM)
    scores = jnp.einsum('rhd,khd->hrk', head_query, head_key, precision=lax.Precision.HIGHEST)
    scores = low_back(scores)
    scores = jnp.where(allowed[None], scores, -1e+30)
    row_max = lax.optimization_barrier(jnp.max(scores, -1, keepdims=True))
    shifted = jnp.exp(scores - row_max)
    attn_probs = low(shifted / lax.optimization_barrier(jnp.sum(shifted, -1, keepdims=True)))
    mixed = jnp.einsum('hrk,khd->rhd', attn_probs, head_value, precision=lax.Precision.HIGHEST)
    return mixed.reshape(row_total, HEADS * HDIM)

def group_forward(params, prompt_rows, cont_rows, encoder_rows, prompt_begin, cont_begin):
    self_proj, self_out, cross_query, cross_kv, cross_out, up_proj, down_proj, vec_bias, up_bias, ln_gain, ln_bias = params
    scale = HDIM ** (-0.5)
    slot_rows = CDEV * CLEN
    block_rows = PDEV + slot_rows
    tokens = jnp.concatenate([prompt_rows, cont_rows.reshape(NCONT * CLEN, D)], 0)
    projected = matmul(tokens, self_proj)
    queries = round_both((projected[:, :D] + vec_bias[0]) * scale)
    key_rows = round_both(projected[:, D:2 * D])
    value_rows = round_both(projected[:, 2 * D:] + vec_bias[1])

    def self_block(block_index):
        prompt_part = lax.dynamic_slice_in_dim(queries, block_index * PDEV, PDEV, 0)
        cont_part = lax.dynamic_slice_in_dim(queries, PROMPT + block_index * slot_rows, slot_rows, 0)
        cont_keys = lax.dynamic_slice_in_dim(key_rows, PROMPT + block_index * slot_rows, slot_rows, 0)
        cont_values = lax.dynamic_slice_in_dim(value_rows, PROMPT + block_index * slot_rows, slot_rows, 0)
        begins = lax.dynamic_slice_in_dim(cont_begin, block_index * CDEV, CDEV, 0)
        allowed = block_mask(block_index, prompt_begin, begins, PDEV, N_CTX, CDEV, CLEN)
        return attend(jnp.concatenate([prompt_part, cont_part], 0), jnp.concatenate([key_rows[:PROMPT], cont_keys], 0), jnp.concatenate([value_rows[:PROMPT], cont_values], 0), allowed)
    mixed = lax.map(jax.checkpoint(self_block), jnp.arange(N_CTX, dtype=jnp.int32))
    attn = jnp.concatenate([mixed[:, :PDEV].reshape(PROMPT, D), mixed[:, PDEV:].reshape(NCONT * CLEN, D)], 0)
    attn = round_both(attn)
    branch_self = low_back(matmul(attn, self_out) + vec_bias[2])
    hidden_one = low(layer_norm(tokens + branch_self, ln_gain[0], ln_bias[0]))
    cross_queries = round_both((matmul(hidden_one, cross_query) + vec_bias[3]) * scale)
    encoder_kv = matmul(encoder_rows, cross_kv)
    enc_keys = round_both(encoder_kv[:, :D])
    enc_values = round_both(encoder_kv[:, D:] + vec_bias[4])
    open_mask = jnp.ones((block_rows, ENC), bool)

    def cross_block(block_queries):
        return attend(block_queries, enc_keys, enc_values, open_mask)
    cross_mixed = lax.map(jax.checkpoint(cross_block), cross_queries.reshape(N_CTX, block_rows, D))
    cross_attn = round_both(cross_mixed.reshape(N_CTX * block_rows, D))
    branch_cross = low_back(matmul(cross_attn, cross_out) + vec_bias[5])
    hidden_two = low(layer_norm(hidden_one + branch_cross, ln_gain[1], ln_bias[1]))
    pre_act = low_back(matmul(hidden_two, up_proj) + up_bias)
    act = low(jax.nn.gelu(pre_act, approximate=False))
    branch_ffn = low_back(matmul(act, down_proj) + vec_bias[6])
    output = layer_norm(hidden_two + branch_ffn, ln_gain[2], ln_bias[2])
    prompt_valid = jnp.arange(PROMPT, dtype=jnp.int32) >= prompt_begin
    places = jnp.arange(CLEN, dtype=jnp.int32)
    cont_valid = (places[None, :] >= cont_begin[:, None]).reshape(NCONT * CLEN)
    valid_rows = jnp.concatenate([prompt_valid, cont_valid]).astype(jnp.float32)
    square_sums = jnp.stack([jnp.sum(valid_rows[:, None] * member * member) for member in (tokens, branch_self, hidden_one, branch_cross, hidden_two, branch_ffn)])
    statistics = square_sums / (jnp.sum(valid_rows) * D)
    return ((output[:PROMPT], output[PROMPT:].reshape(NCONT, CLEN, D)), statistics)

def reference(prompt_in, cont_in, encoder, prompt_start, cont_start, self_proj, self_out, cross_query, cross_kv, cross_out, up_proj, down_proj, vec_bias, up_bias, ln_gain, ln_bias, prompt_cot, cont_cot):
    params = tuple((member.astype(jnp.float32) for member in (self_proj, self_out, cross_query, cross_kv, cross_out, up_proj, down_proj, vec_bias, up_bias, ln_gain, ln_bias)))

    def forward(weights, prompt_rows, cont_rows, encoder_rows):

        def one_group(group_args):
            return group_forward(weights, group_args[0], group_args[1], group_args[2], group_args[3], group_args[4])
        outputs, statistics = lax.map(one_group, (prompt_rows, cont_rows, encoder_rows, prompt_start, cont_start))
        return (outputs, statistics)
    outputs, pull_back, statistics = jax.vjp(forward, params, prompt_in.astype(jnp.float32), cont_in.astype(jnp.float32), encoder.astype(jnp.float32), has_aux=True)
    param_grads, prompt_grad, cont_grad, encoder_grad = pull_back((prompt_cot.astype(jnp.float32), cont_cot.astype(jnp.float32)))
    return (outputs[0].astype(jnp.bfloat16), outputs[1].astype(jnp.bfloat16), prompt_grad, cont_grad, encoder_grad, param_grads[0], param_grads[1], param_grads[2], param_grads[3], param_grads[4], param_grads[5], param_grads[6], param_grads[7], param_grads[8], param_grads[9], param_grads[10], statistics)
```

```python
import functools

import jax
import jax.numpy as jnp
from jax import lax
from jax.experimental import pallas as pl
from jax.experimental.pallas import tpu as pltpu
from jax.sharding import Mesh
from jax.sharding import PartitionSpec as P

HEADS = 16
HDIM = 64
MASKED = -1e30


def product(first_mat, second_mat):
    return jnp.dot(first_mat, second_mat, preferred_element_type=jnp.float32)


def product_tn(first_mat, second_mat):
    return lax.dot_general(
        first_mat, second_mat, (((0,), (0,)), ((), ())), preferred_element_type=jnp.float32
    )


def product_nt(first_mat, second_mat):
    return lax.dot_general(
        first_mat, second_mat, (((1,), (1,)), ((), ())), preferred_element_type=jnp.float32
    )


def bias_fill(sc_ref, prompt_bias, own_bias, flip):
    begin, cont_begin, block = sc_ref[0], sc_ref[1], sc_ref[2]
    q_dim, k_dim = (1, 0) if flip else (0, 1)
    shape = prompt_bias.shape
    rows = shape[q_dim]
    spot = lax.broadcasted_iota(jnp.int32, shape, q_dim) + block * rows
    key = lax.broadcasted_iota(jnp.int32, shape, k_dim)
    seen = (key <= spot) & ((key >= begin) | (key == spot))
    prompt_bias[...] = jnp.where(seen, 0.0, MASKED)
    shape = own_bias.shape
    spot = lax.broadcasted_iota(jnp.int32, shape, q_dim)
    key = lax.broadcasted_iota(jnp.int32, shape, k_dim)
    seen = (key <= spot) & ((key >= cont_begin) | (key == spot))
    own_bias[...] = jnp.where(seen, 0.0, MASKED)


def self_plan(prompt_rows, prompt_len, slot_len):
    step = slot_len // 2
    return (
        (0, prompt_rows, ((0, prompt_len, "prompt"),)),
        (prompt_rows, step, ((0, prompt_len, "start"), (1, step, "own"))),
        (prompt_rows + step, slot_len - step, ((0, prompt_len, "start"), (1, slot_len, "own"))),
    )


def cross_plan(row_total, key_total, step):
    return tuple(
        (at, min(step, row_total - at), ((0, key_total, None),)) for at in range(0, row_total, step)
    )


def head_lanes(head):
    lane = lax.broadcasted_iota(jnp.int32, (1, 2 * HDIM), 1)
    return (lane >= head * HDIM) & (lane < (head + 1) * HDIM)


def only(block, lanes):
    return jnp.where(lanes, block, jnp.zeros_like(block))


def fwd_kernel(plan, masked, slot_at, *refs):
    n_seg = 2 if masked else 1
    if masked:
        sc_ref, refs = refs[0], refs[1:]
    q_ref = refs[0]
    k_refs, v_refs = refs[1 : 1 + n_seg], refs[1 + n_seg : 1 + 2 * n_seg]
    o_ref, lse_ref = refs[1 + 2 * n_seg : 3 + 2 * n_seg]
    pair = pl.program_id(0)
    if masked:
        prompt_bias, own_bias = refs[3 + 2 * n_seg :]

        @pl.when(pair == 0)
        def _():
            bias_fill(sc_ref, prompt_bias, own_bias, False)

    out_lane = lax.broadcasted_iota(jnp.int32, (1, 128), 1)
    for q_at, q_n, parts in plan:
        rows = slice(q_at, q_at + q_n)
        q_blk = q_ref[rows, :]
        mixed_pair = None
        for head in (0, 1):
            lanes = head_lanes(head)
            q_one = only(q_blk, lanes)
            scores = []
            for seg, k_n, kind in parts:
                part = product_nt(q_one, k_refs[seg][:k_n, :])
                if kind == "prompt":
                    part = part + prompt_bias[...]
                elif kind == "own":
                    at = q_at - slot_at
                    part = part + own_bias[at : at + q_n, :k_n]
                elif kind == "start":
                    key = lax.broadcasted_iota(jnp.int32, (1, 128), 1)
                    first = jnp.where(key >= sc_ref[0], part[:, :128], MASKED)
                    part = jnp.concatenate([first, part[:, 128:]], 1)
                scores.append(part)
            row_max = functools.reduce(
                jnp.maximum, [jnp.max(part, 1, keepdims=True) for part in scores]
            )
            totals, mixed = 0.0, 0.0
            for part, (seg, k_n, _) in zip(scores, parts):
                shifted = jnp.exp(part - row_max)
                totals = totals + jnp.sum(shifted, 1, keepdims=True)
                mixed = mixed + product(shifted.astype(jnp.bfloat16), v_refs[seg][:k_n, :])
            mixed = mixed / totals
            mixed_pair = mixed if head == 0 else jnp.where(lanes, mixed, mixed_pair)
            lse = row_max + jnp.log(totals)
            lse_ref[rows, :] = jnp.where(out_lane == 2 * pair + head, lse, lse_ref[rows, :])
        o_ref[rows, :] = mixed_pair.astype(jnp.bfloat16)


def accumulate(total_ref, keys, done, part):
    known = min(max(done - keys.start, 0), keys.stop - keys.start)
    if known:
        total_ref[keys.start : keys.start + known, :] += part[:known]
    if known < keys.stop - keys.start:
        total_ref[keys.start + known : keys.stop, :] = part[known:]


def bwd_kernel(plan, masked, slot_at, key_step, *refs):
    n_seg = 2 if masked else 1
    if masked:
        sc_ref, refs = refs[0], refs[1:]
    q_ref, g_ref, o_ref, lse_ref = refs[:4]
    k_refs, v_refs = refs[4 : 4 + n_seg], refs[4 + n_seg : 4 + 2 * n_seg]
    outs = refs[4 + 2 * n_seg :]
    dq_ref, dk_refs, dv_refs = outs[0], outs[1 : 1 + n_seg], outs[1 + n_seg : 1 + 2 * n_seg]
    scratch = outs[1 + 2 * n_seg :]
    dk_acc, dv_acc = scratch[:n_seg], scratch[n_seg : 2 * n_seg]
    pair = pl.program_id(0)
    if masked:
        prompt_bias, own_bias = scratch[2 * n_seg :]

        @pl.when(pair == 0)
        def _():
            bias_fill(sc_ref, prompt_bias, own_bias, True)

    done = [0] * n_seg
    picks = jnp.concatenate(
        [only(jnp.ones((1, 2 * HDIM), jnp.float32), head_lanes(h)) for h in (0, 1)]
        + [jnp.zeros((6, 2 * HDIM), jnp.float32)],
        0,
    )
    for q_at, q_n, parts in plan:
        rows = slice(q_at, q_at + q_n)
        q_blk, g_blk = q_ref[rows, :], g_ref[rows, :]
        inner = lax.dot_general(
            picks,
            g_blk.astype(jnp.float32) * o_ref[rows, :].astype(jnp.float32),
            (((1,), (1,)), ((), ())),
            precision=lax.Precision.HIGHEST,
            preferred_element_type=jnp.float32,
        )
        dq = 0.0
        for head in (0, 1):
            lanes = head_lanes(head)
            q_one, g_one = only(q_blk, lanes), only(g_blk, lanes)
            lse = lse_ref[0, head : head + 1, rows]
            row_inner = inner[head : head + 1, :]
            for seg, k_n, kind in parts:
                for at in range(0, k_n, key_step):
                    keys = slice(at, min(at + key_step, k_n))
                    k_one = only(k_refs[seg][keys, :], lanes)
                    scores = product_nt(k_one, q_blk)
                    if kind == "prompt":
                        scores = scores + prompt_bias[keys, :]
                    elif kind == "own":
                        q_off = q_at - slot_at
                        scores = scores + own_bias[keys, q_off : q_off + q_n]
                    elif kind == "start" and at == 0:
                        key = lax.broadcasted_iota(jnp.int32, (128, 1), 0)
                        first = jnp.where(key >= sc_ref[0], scores[:128, :], MASKED)
                        scores = jnp.concatenate([first, scores[128:, :]], 0)
                    probs = jnp.exp(scores - lse)
                    grad_probs = product_nt(v_refs[seg][keys, :], g_one)
                    grad_scores = (probs * (grad_probs - row_inner)).astype(jnp.bfloat16)
                    add_v = product(probs.astype(jnp.bfloat16), g_one)
                    add_k = product(grad_scores, q_one)
                    accumulate(dv_acc[seg], keys, done[seg], add_v)
                    accumulate(dk_acc[seg], keys, done[seg], add_k)
                    dq = dq + product_tn(grad_scores, k_one)
                done[seg] = max(done[seg], k_n)
        dq_ref[rows, :] = dq.astype(jnp.bfloat16)
    for seg in range(n_seg):
        dk_refs[seg][...] = dk_acc[seg][...].astype(jnp.bfloat16)
        dv_refs[seg][...] = dv_acc[seg][...].astype(jnp.bfloat16)


VMEM_LIMIT = 48 * 1024 * 1024


def pair_spec(rows, shift=0):
    return pl.BlockSpec((rows, 2 * HDIM), lambda i: (0, i + shift))


def attend_forward(scalars, queries, kv_list, plan, slot_at):
    masked = scalars is not None
    row_total, width = queries.shape
    pairs = width // (2 * HDIM)
    scratch = []
    if masked:
        prompt_len, slot_len = kv_list[0].shape[0], kv_list[1].shape[0]
        scratch = [
            pltpu.VMEM((slot_at, prompt_len), jnp.float32),
            pltpu.VMEM((slot_len, slot_len), jnp.float32),
        ]
    area = sum(q_n * k_n for _, q_n, parts in plan for _, k_n, _ in parts)
    return pl.pallas_call(
        functools.partial(fwd_kernel, plan, masked, slot_at),
        grid=(pairs,),
        in_specs=([pl.BlockSpec(memory_space=pltpu.SMEM)] if masked else [])
        + [pair_spec(row_total)]
        + [pair_spec(kv.shape[0]) for kv in kv_list]
        + [pair_spec(kv.shape[0], pairs) for kv in kv_list],
        out_specs=[pair_spec(row_total), pl.BlockSpec((row_total, 128), lambda i: (0, 0))],
        out_shape=[
            jax.ShapeDtypeStruct((row_total, width), jnp.bfloat16),
            jax.ShapeDtypeStruct((row_total, 128), jnp.float32),
        ],
        scratch_shapes=scratch,
        compiler_params=pltpu.CompilerParams(
            dimension_semantics=("arbitrary",), vmem_limit_bytes=VMEM_LIMIT
        ),
        cost_estimate=pl.CostEstimate(
            flops=4 * area * HEADS * 128,
            bytes_accessed=4 * row_total * width + sum(2 * kv.size for kv in kv_list),
            transcendentals=area * HEADS,
        ),
        name="attend_forward",
    )(*([scalars] if masked else []), queries, *kv_list, *kv_list)


def attend_backward(scalars, queries, grads, mixed, log_totals, kv_list, plan, slot_at, key_step):
    masked = scalars is not None
    row_total, width = queries.shape
    pairs = width // (2 * HDIM)
    lse = log_totals[:, :HEADS].T.reshape(pairs, 2, row_total)
    scratch = [pltpu.VMEM((kv.shape[0], 2 * HDIM), jnp.float32) for kv in kv_list] * 2
    if masked:
        prompt_len, slot_len = kv_list[0].shape[0], kv_list[1].shape[0]
        scratch += [
            pltpu.VMEM((prompt_len, slot_at), jnp.float32),
            pltpu.VMEM((slot_len, slot_len), jnp.float32),
        ]
    area = sum(q_n * k_n for _, q_n, parts in plan for _, k_n, _ in parts)
    n_seg = len(kv_list)
    outs = pl.pallas_call(
        functools.partial(bwd_kernel, plan, masked, slot_at, key_step),
        grid=(pairs,),
        in_specs=([pl.BlockSpec(memory_space=pltpu.SMEM)] if masked else [])
        + [pair_spec(row_total)] * 3
        + [pl.BlockSpec((1, 2, row_total), lambda i: (i, 0, 0))]
        + [pair_spec(kv.shape[0]) for kv in kv_list]
        + [pair_spec(kv.shape[0], pairs) for kv in kv_list],
        out_specs=[pair_spec(row_total)] + [pair_spec(kv.shape[0]) for kv in kv_list] * 2,
        out_shape=[jax.ShapeDtypeStruct((row_total, width), jnp.bfloat16)]
        + [jax.ShapeDtypeStruct((kv.shape[0], width), jnp.bfloat16) for kv in kv_list] * 2,
        scratch_shapes=scratch,
        compiler_params=pltpu.CompilerParams(
            dimension_semantics=("arbitrary",), vmem_limit_bytes=VMEM_LIMIT
        ),
        cost_estimate=pl.CostEstimate(
            flops=10 * area * HEADS * 128,
            bytes_accessed=8 * row_total * width + sum(4 * kv.size for kv in kv_list),
            transcendentals=area * HEADS,
        ),
        name="attend_backward",
    )(*([scalars] if masked else []), queries, grads, mixed, lse, *kv_list, *kv_list)
    return outs[0], outs[1 : 1 + n_seg], outs[1 + n_seg :]


def column_sum(matrix):
    return jnp.sum(matrix.astype(jnp.float32), 0)


def layer_norm(residual, gain_vec, shift_vec):
    row_mean = jnp.mean(residual, -1, keepdims=True)
    centred = residual - row_mean
    row_var = jnp.mean(centred * centred, -1, keepdims=True)
    return centred * lax.rsqrt(row_var + 1e-05) * gain_vec + shift_vec


def layer_norm_back(residual, gain_vec, grad):
    row_mean = jnp.mean(residual, -1, keepdims=True)
    centred = residual - row_mean
    row_var = jnp.mean(centred * centred, -1, keepdims=True)
    inverse = lax.rsqrt(row_var + 1e-05)
    xhat = centred * inverse
    dx = grad * gain_vec
    inner = dx - jnp.mean(dx, -1, keepdims=True) - xhat * jnp.mean(dx * xhat, -1, keepdims=True)
    return inner * inverse, jnp.sum(grad * xhat, 0), jnp.sum(grad, 0)


SWAP = ((0, 1), (1, 0))


def swap(value, axis):
    return lax.ppermute(value, axis, SWAP)


def xor_perm(count, shift):
    return tuple((i, i ^ shift) for i in range(count))


def reduce_stages(part, names, order):
    names = list(names)
    for axis in order:
        dim = names.index(axis)
        count = part.shape[dim]
        here = lax.axis_index(axis)
        total = lax.dynamic_index_in_dim(part, here, dim, keepdims=False).astype(jnp.float32)
        for shift in range(1, count):
            other = lax.dynamic_index_in_dim(part, here ^ shift, dim, keepdims=False)
            came = lax.ppermute(other, axis, xor_perm(count, shift))
            total = total + came.astype(jnp.float32)
        names.pop(dim)
        part = total if not names else total.astype(jnp.bfloat16)
    return part


class Links:
    def __init__(self, mesh):
        self.fast = dict(mesh.shape) == {"fsdp": 4, "ctx": 8}
        if self.fast:
            self.mesh = Mesh(mesh.devices.reshape(2, 2, 4, 2), ("x", "c", "z", "y"))
            self.rows, self.ctx = ("x", "c"), ("z", "y")
        else:
            self.mesh, self.rows, self.ctx = mesh, ("fsdp",), ("ctx",)
        self.every = self.rows + self.ctx

    def gather(self, value, axes):
        return lax.all_gather(value, axes, axis=0, tiled=True)

    def scatter(self, part, order):
        part = part.astype(jnp.bfloat16)
        if not self.fast:
            return lax.psum_scatter(part, self.every, scatter_dimension=0, tiled=True).astype(
                jnp.float32
            )
        part = part.reshape(2, 2, 4, 2, part.shape[0] // 32, part.shape[1])
        return reduce_stages(part, "xczy", order)

    def scatter_ctx(self, part, order):
        part = part.astype(jnp.bfloat16)
        if not self.fast:
            return lax.psum_scatter(part, self.ctx, scatter_dimension=0, tiled=True).astype(
                jnp.float32
            )
        part = part.reshape(4, 2, part.shape[0] // 8, part.shape[1])
        return reduce_stages(part, "zy", order)

    def total(self, value, axes):
        if not self.fast:
            return lax.psum(value, axes)
        for axis in axes:
            count = 4 if axis == "z" else 2
            value = value + sum(
                lax.ppermute(value, axis, xor_perm(count, shift)) for shift in range(1, count)
            )
        return value


def body(
    links,
    prompt_in,
    cont_in,
    encoder,
    prompt_start,
    cont_start,
    self_proj,
    self_out,
    cross_query,
    cross_kv,
    cross_out,
    up_proj,
    down_proj,
    vec_bias,
    up_bias,
    ln_gain,
    ln_bias,
    prompt_cot,
    cont_cot,
):
    f32, bf16 = jnp.float32, jnp.bfloat16
    shard, width = self_out.shape
    prompt_rows, slot_len = prompt_in.shape[1], cont_in.shape[2]
    block_index = lax.axis_index(links.ctx)
    ctx_count = lax.axis_size(links.ctx)
    prompt_len = prompt_rows * ctx_count
    enc_rows = encoder.shape[1]
    hidden = up_bias.shape[0] // shard
    scale = HDIM ** (-0.5)

    small = jnp.concatenate(
        [vec_bias.T, ln_gain.T, ln_bias.T, up_bias.reshape(hidden, shard).T], 1
    )
    small = jnp.pad(small, ((0, 0), (0, 128 - small.shape[1])))
    inputs_all = links.gather(jnp.concatenate([prompt_in[0], encoder[0]], 0), links.ctx)
    inputs_all = inputs_all.reshape(ctx_count, prompt_rows + enc_rows, width)
    prompt_all = inputs_all[:, :prompt_rows].reshape(prompt_len, width)
    enc_all = inputs_all[:, prompt_rows:].reshape(enc_rows * ctx_count, width)
    first = links.gather(jnp.concatenate([self_proj, small], 1), links.every)
    second = links.gather(
        jnp.concatenate([self_out, cross_query, cross_kv, cross_out], 1), links.every
    )
    w_up = links.gather(up_proj, links.every)
    w_down = links.gather(down_proj, links.every)
    w_q, w_kv = first[:, :width], first[:, width : 3 * width]
    w_so, w_cq = second[:, :width], second[:, width : 2 * width]
    w_ckv, w_co = second[:, 2 * width : 4 * width], second[:, 4 * width :]
    small = first[:, 3 * width :].astype(f32).T
    biases, gains, shifts = small[:7], small[7:10], small[10:13]
    hidden_bias = (
        small[13 : 13 + hidden]
        .reshape(hidden, width // shard, shard)
        .transpose(1, 0, 2)
        .reshape(hidden * width)
    )

    every_begin = cont_start[0]
    own_begin = lax.dynamic_index_in_dim(every_begin, block_index, 0, keepdims=False)
    scalars = jnp.stack([prompt_start[0], own_begin, block_index.astype(jnp.int32)])
    cont_rows = cont_in[0, 0]
    tokens = jnp.concatenate([prompt_in[0], cont_rows], 0)
    row_total = tokens.shape[0]
    row_spot = jnp.arange(row_total, dtype=jnp.int32)
    valid_rows = jnp.where(
        row_spot < prompt_rows,
        block_index * prompt_rows + row_spot >= prompt_start[0],
        row_spot - prompt_rows >= own_begin,
    ).astype(f32)[:, None]
    valid_count = (prompt_len - prompt_start[0] + jnp.sum(slot_len - every_begin)).astype(f32)

    kv_bias = jnp.concatenate([jnp.zeros((width,), f32), biases[1]])
    queries = ((product(tokens, w_q) + biases[0]) * scale).astype(bf16)
    prompt_kv = (product(prompt_all, w_kv) + kv_bias).astype(bf16)
    cont_kv = (product(cont_rows, w_kv) + kv_bias).astype(bf16)
    plan = self_plan(prompt_rows, prompt_len, slot_len)
    attn, self_log = attend_forward(scalars, queries, [prompt_kv, cont_kv], plan, prompt_rows)
    branch_self = product(attn, w_so) + biases[2]
    resid_one = tokens.astype(f32) + branch_self
    hidden_one = layer_norm(resid_one, gains[0], shifts[0]).astype(bf16)

    enc_bias = jnp.concatenate([jnp.zeros((width,), f32), biases[4]])
    enc_kv = (product(enc_all, w_ckv) + enc_bias).astype(bf16)
    cross_queries = ((product(hidden_one, w_cq) + biases[3]) * scale).astype(bf16)
    enc_len = enc_all.shape[0]
    cross_attn, cross_log = attend_forward(
        None, cross_queries, [enc_kv], cross_plan(row_total, enc_len, 320), 0
    )
    branch_cross = product(cross_attn, w_co) + biases[5]
    resid_two = hidden_one.astype(f32) + branch_cross
    hidden_two = layer_norm(resid_two, gains[1], shifts[1]).astype(bf16)

    pre_act = product(hidden_two, w_up) + hidden_bias
    half = 0.5 * (1.0 + lax.erf(pre_act * (0.5**0.5)))
    act = (pre_act * half).astype(bf16)
    slope = (half + pre_act * jnp.exp(-0.5 * pre_act * pre_act) * 0.3989422804014327).astype(bf16)
    branch_ffn = product(act, w_down) + biases[6]
    resid_three = hidden_two.astype(f32) + branch_ffn
    output = layer_norm(resid_three, gains[2], shifts[2]).astype(bf16)

    members = (tokens, branch_self, hidden_one, branch_cross, hidden_two, branch_ffn)
    squares = jnp.stack(
        [jnp.sum(valid_rows * jnp.square(member.astype(f32))) for member in members]
    )
    squares = links.total(jnp.pad(squares[None], ((0, 7), (0, 122))), links.ctx)[0, :6]
    statistics = (squares / (valid_count * width))[None]

    grad_out = jnp.concatenate([prompt_cot[0], cont_cot[0, 0]], 0).astype(f32)
    grad_three, gain_three, shift_three = layer_norm_back(resid_three, gains[2], grad_out)
    grad_ffn = grad_three.astype(bf16)
    down_total = links.scatter(product_tn(act, grad_ffn), "cxyz")
    grad_pre = (product_nt(grad_ffn, w_down) * slope.astype(f32)).astype(bf16)
    up_total = links.scatter(product_tn(hidden_two, grad_pre), "cyxz")
    grad_hidden_two = grad_three + product_nt(grad_pre, w_up)
    grad_two, gain_two, shift_two = layer_norm_back(resid_two, gains[1], grad_hidden_two)
    grad_cross = grad_two.astype(bf16)
    co_total = links.scatter(product_tn(cross_attn, grad_cross), "czxy")
    grad_cattn = product_nt(grad_cross, w_co).astype(bf16)
    cross_gq, cross_gk, cross_gv = attend_backward(
        None,
        cross_queries,
        grad_cattn,
        cross_attn,
        cross_log,
        [enc_kv],
        cross_plan(row_total, enc_len, 384),
        0,
        512,
    )
    grad_cq = (cross_gq.astype(f32) * scale).astype(bf16)
    enc_gkv = jnp.concatenate([cross_gk[0], cross_gv[0]], 1)
    cq_total = links.scatter(product_tn(hidden_one, grad_cq), "cxyz")
    ckv_total = links.scatter(product_tn(enc_all, enc_gkv), "cyxz")
    encoder_grad = links.scatter_ctx(product_nt(enc_gkv, w_ckv), "zy")[None]
    grad_hidden_one = grad_two + product_nt(grad_cq, w_cq)
    grad_one, gain_one, shift_one = layer_norm_back(resid_one, gains[0], grad_hidden_one)
    grad_self = grad_one.astype(bf16)
    so_total = links.scatter(product_tn(attn, grad_self), "cxyz")
    grad_attn = product_nt(grad_self, w_so).astype(bf16)
    self_gq, self_gk, self_gv = attend_backward(
        scalars,
        queries,
        grad_attn,
        attn,
        self_log,
        [prompt_kv, cont_kv],
        plan,
        prompt_rows,
        1024,
    )
    grad_q = (self_gq.astype(f32) * scale).astype(bf16)
    prompt_gkv = jnp.concatenate([self_gk[0], self_gv[0]], 1)
    cont_gkv = jnp.concatenate([self_gk[1], self_gv[1]], 1)
    prompt_back = product_nt(prompt_gkv, w_kv)
    half_width = width // 2
    prompt_back = jnp.concatenate(
        [
            links.scatter_ctx(prompt_back[:, :half_width], "yz"),
            links.scatter_ctx(prompt_back[:, half_width:], "zy"),
        ],
        1,
    )
    sin_q = product_tn(tokens, grad_q)
    sin_kv = product_tn(prompt_all, prompt_gkv) + product_tn(cont_rows, cont_gkv)
    sin_total = jnp.concatenate(
        [
            links.scatter(sin_q, "cxyz"),
            links.scatter(sin_kv[:, :width], "cyxz"),
            links.scatter(sin_kv[:, width:], "czxy"),
        ],
        1,
    )
    input_grad = grad_one + product_nt(grad_q, w_q)
    prompt_grad = (input_grad[:prompt_rows] + prompt_back)[None]
    cont_grad = (input_grad[prompt_rows:] + product_nt(cont_gkv, w_kv))[None, None]

    up_bias_part = column_sum(grad_pre).reshape(width // shard, hidden, shard)
    small_part = jnp.concatenate(
        [
            jnp.stack(
                [
                    column_sum(grad_q),
                    column_sum(self_gv[0]) + column_sum(self_gv[1]),
                    column_sum(grad_self),
                    column_sum(grad_cq),
                    column_sum(cross_gv[0]),
                    column_sum(grad_cross),
                    column_sum(grad_ffn),
                    gain_one,
                    gain_two,
                    gain_three,
                    shift_one,
                    shift_two,
                    shift_three,
                ]
            ),
            up_bias_part.transpose(1, 0, 2).reshape(hidden, width),
        ],
        0,
    )
    small_total = links.total(small_part, links.every)
    at = lax.axis_index(links.every) * shard
    small_total = lax.dynamic_slice_in_dim(small_total, at, shard, 1)
    bias_total, gain_total, shift_total = small_total[:7], small_total[7:10], small_total[10:13]
    up_bias_total = small_total[13 : 13 + hidden].reshape(hidden * shard)
    return (
        output[:prompt_rows][None],
        output[prompt_rows:][None, None],
        prompt_grad,
        cont_grad,
        encoder_grad,
        sin_total,
        so_total,
        cq_total,
        ckv_total,
        co_total,
        up_total,
        down_total,
        bias_total,
        up_bias_total,
        gain_total,
        shift_total,
        statistics,
    )


def solution(mesh):
    links = Links(mesh)
    fs, ctx, every = links.rows, links.ctx, links.every
    group = P(fs, ctx, None)
    slots = P(fs, ctx, None, None)
    weight = P(every, None)
    vectors = P(None, every)
    return jax.shard_map(
        functools.partial(body, links),
        mesh=links.mesh,
        in_specs=(group, slots, group, P(fs), P(fs, None))
        + (weight,) * 7
        + (vectors, P(every), vectors, vectors, group, slots),
        out_specs=(group, slots, group, slots, group)
        + (weight,) * 7
        + (vectors, P(every), vectors, vectors, P(fs, None)),
        check_vma=False,
    )
```

```python
import functools
import itertools

import jax
import jax.numpy as jnp
from jax import lax
from jax.experimental import pallas as pl
from jax.experimental.pallas import tpu as pltpu
from jax.sharding import Mesh
from jax.sharding import PartitionSpec as P

HEADS = 16
HDIM = 64
MASKED = -1e30


def product(first_mat, second_mat):
    return jnp.dot(first_mat, second_mat, preferred_element_type=jnp.float32)


def product_tn(first_mat, second_mat):
    return lax.dot_general(
        first_mat, second_mat, (((0,), (0,)), ((), ())), preferred_element_type=jnp.float32
    )


def product_nt(first_mat, second_mat):
    return lax.dot_general(
        first_mat, second_mat, (((1,), (1,)), ((), ())), preferred_element_type=jnp.float32
    )


def bias_fill(sc_ref, prompt_bias, own_bias, flip, segs=(0, 1)):
    begin, cont_begin, block = sc_ref[0], sc_ref[1], sc_ref[2]
    q_dim, k_dim = (1, 0) if flip else (0, 1)
    if 0 in segs:
        shape = prompt_bias.shape
        rows = shape[q_dim]
        spot = lax.broadcasted_iota(jnp.int32, shape, q_dim) + block * rows
        key = lax.broadcasted_iota(jnp.int32, shape, k_dim)
        seen = (key <= spot) & ((key >= begin) | (key == spot))
        prompt_bias[...] = jnp.where(seen, 0.0, MASKED)
    if 1 in segs:
        shape = own_bias.shape
        spot = lax.broadcasted_iota(jnp.int32, shape, q_dim)
        key = lax.broadcasted_iota(jnp.int32, shape, k_dim)
        seen = (key <= spot) & ((key >= cont_begin) | (key == spot))
        own_bias[...] = jnp.where(seen, 0.0, MASKED)


def self_plan(prompt_rows, prompt_len, slot_len):
    step = slot_len // 2
    return (
        (0, prompt_rows, ((0, prompt_len, "prompt"),)),
        (prompt_rows, step, ((0, prompt_len, "start"), (1, step, "own"))),
        (prompt_rows + step, slot_len - step, ((0, prompt_len, "start"), (1, slot_len, "own"))),
    )


def cross_plan(row_total, key_total, step):
    return tuple(
        (at, min(step, row_total - at), ((0, key_total, None),)) for at in range(0, row_total, step)
    )


def head_lanes(head):
    lane = lax.broadcasted_iota(jnp.int32, (1, 2 * HDIM), 1)
    return (lane >= head * HDIM) & (lane < (head + 1) * HDIM)


def only(block, lanes):
    return jnp.where(lanes, block, jnp.zeros_like(block))


def fwd_kernel(plan, masked, slot_at, *refs):
    n_seg = 2 if masked else 1
    if masked:
        sc_ref, refs = refs[0], refs[1:]
    q_ref = refs[0]
    k_refs, v_refs = refs[1 : 1 + n_seg], refs[1 + n_seg : 1 + 2 * n_seg]
    o_ref, lse_ref = refs[1 + 2 * n_seg : 3 + 2 * n_seg]
    pair = pl.program_id(0)
    if masked:
        prompt_bias, own_bias = refs[3 + 2 * n_seg :]

        @pl.when(pair == 0)
        def _():
            bias_fill(sc_ref, prompt_bias, own_bias, False)

    out_lane = lax.broadcasted_iota(jnp.int32, (1, 128), 1)
    for q_at, q_n, parts in plan:
        rows = slice(q_at, q_at + q_n)
        q_blk = q_ref[rows, :]
        mixed_pair = None
        for head in (0, 1):
            lanes = head_lanes(head)
            q_one = only(q_blk, lanes)
            scores = []
            for seg, k_n, kind in parts:
                part = product_nt(q_one, k_refs[seg][:k_n, :])
                if kind == "prompt":
                    part = part + prompt_bias[...]
                elif kind == "own":
                    at = q_at - slot_at
                    part = part + own_bias[at : at + q_n, :k_n]
                elif kind == "start":
                    key = lax.broadcasted_iota(jnp.int32, (1, 128), 1)
                    first = jnp.where(key >= sc_ref[0], part[:, :128], MASKED)
                    part = jnp.concatenate([first, part[:, 128:]], 1)
                scores.append(part)
            row_max = functools.reduce(
                jnp.maximum, [jnp.max(part, 1, keepdims=True) for part in scores]
            )
            totals, mixed = 0.0, 0.0
            for part, (seg, k_n, _) in zip(scores, parts):
                shifted = jnp.exp(part - row_max)
                totals = totals + jnp.sum(shifted, 1, keepdims=True)
                mixed = mixed + product(shifted.astype(jnp.bfloat16), v_refs[seg][:k_n, :])
            mixed = mixed / totals
            mixed_pair = mixed if head == 0 else jnp.where(lanes, mixed, mixed_pair)
            lse = row_max + jnp.log(totals)
            lse_ref[rows, :] = jnp.where(out_lane == 2 * pair + head, lse, lse_ref[rows, :])
        o_ref[rows, :] = mixed_pair.astype(jnp.bfloat16)


def accumulate(total_ref, keys, done, part):
    known = min(max(done - keys.start, 0), keys.stop - keys.start)
    if known:
        total_ref[keys.start : keys.start + known, :] += part[:known]
    if known < keys.stop - keys.start:
        total_ref[keys.start + known : keys.stop, :] = part[known:]


def bwd_kernel(plan, masked, slot_at, key_step, segs, onto, *refs):
    n_seg = len(segs)
    if masked:
        sc_ref, refs = refs[0], refs[1:]
    q_ref, g_ref, o_ref, lse_ref = refs[:4]
    k_refs, v_refs = refs[4 : 4 + n_seg], refs[4 + n_seg : 4 + 2 * n_seg]
    outs = refs[4 + 2 * n_seg :]
    if onto:
        dq_in, outs = outs[0], outs[1:]
        dq_in_rows = slice(0, plan[0][0])
        outs[0][dq_in_rows, :] = dq_in[dq_in_rows, :].astype(outs[0].dtype)
    dq_ref, dk_refs, dv_refs = outs[0], outs[1 : 1 + n_seg], outs[1 + n_seg : 1 + 2 * n_seg]
    scratch = outs[1 + 2 * n_seg :]
    dk_acc, dv_acc = scratch[:n_seg], scratch[n_seg : 2 * n_seg]
    pair = pl.program_id(0)
    if masked:
        prompt_bias, own_bias = scratch[2 * n_seg :]

        @pl.when(pair == 0)
        def _():
            bias_fill(sc_ref, prompt_bias, own_bias, True, segs)

    done = [0] * n_seg
    picks = jnp.concatenate(
        [only(jnp.ones((1, 2 * HDIM), jnp.float32), head_lanes(h)) for h in (0, 1)]
        + [jnp.zeros((6, 2 * HDIM), jnp.float32)],
        0,
    )
    for q_at, q_n, parts in plan:
        rows = slice(q_at, q_at + q_n)
        q_blk, g_blk = q_ref[rows, :], g_ref[rows, :]
        inner = lax.dot_general(
            picks,
            g_blk.astype(jnp.float32) * o_ref[rows, :].astype(jnp.float32),
            (((1,), (1,)), ((), ())),
            precision=lax.Precision.HIGHEST,
            preferred_element_type=jnp.float32,
        )
        dq = dq_in[rows, :] if onto else 0.0
        for head in (0, 1):
            lanes = head_lanes(head)
            q_one, g_one = only(q_blk, lanes), only(g_blk, lanes)
            lse = lse_ref[0, head : head + 1, rows]
            row_inner = inner[head : head + 1, :]
            for which, k_n, kind in parts:
                seg = segs.index(which)
                for at in range(0, k_n, key_step):
                    keys = slice(at, min(at + key_step, k_n))
                    k_one = only(k_refs[seg][keys, :], lanes)
                    scores = product_nt(k_one, q_blk)
                    if kind == "prompt":
                        scores = scores + prompt_bias[keys, :]
                    elif kind == "own":
                        q_off = q_at - slot_at
                        scores = scores + own_bias[keys, q_off : q_off + q_n]
                    elif kind == "start" and at == 0:
                        key = lax.broadcasted_iota(jnp.int32, (128, 1), 0)
                        first = jnp.where(key >= sc_ref[0], scores[:128, :], MASKED)
                        scores = jnp.concatenate([first, scores[128:, :]], 0)
                    probs = jnp.exp(scores - lse)
                    grad_probs = product_nt(v_refs[seg][keys, :], g_one)
                    grad_scores = (probs * (grad_probs - row_inner)).astype(jnp.bfloat16)
                    add_v = product(probs.astype(jnp.bfloat16), g_one)
                    add_k = product(grad_scores, q_one)
                    accumulate(dv_acc[seg], keys, done[seg], add_v)
                    accumulate(dk_acc[seg], keys, done[seg], add_k)
                    dq = dq + product_tn(grad_scores, k_one)
                done[seg] = max(done[seg], k_n)
        dq_ref[rows, :] = dq.astype(dq_ref.dtype)
    for seg in range(n_seg):
        dk_refs[seg][...] = dk_acc[seg][...].astype(jnp.bfloat16)
        dv_refs[seg][...] = dv_acc[seg][...].astype(jnp.bfloat16)


VMEM_LIMIT = 48 * 1024 * 1024


def pair_spec(rows, shift=0):
    return pl.BlockSpec((rows, 2 * HDIM), lambda i: (0, i + shift))


def attend_forward(scalars, queries, kv_list, plan, slot_at):
    masked = scalars is not None
    row_total, width = queries.shape
    pairs = width // (2 * HDIM)
    scratch = []
    if masked:
        prompt_len, slot_len = kv_list[0].shape[0], kv_list[1].shape[0]
        scratch = [
            pltpu.VMEM((slot_at, prompt_len), jnp.float32),
            pltpu.VMEM((slot_len, slot_len), jnp.float32),
        ]
    area = sum(q_n * k_n for _, q_n, parts in plan for _, k_n, _ in parts)
    return pl.pallas_call(
        functools.partial(fwd_kernel, plan, masked, slot_at),
        grid=(pairs,),
        in_specs=([pl.BlockSpec(memory_space=pltpu.SMEM)] if masked else [])
        + [pair_spec(row_total)]
        + [pair_spec(kv.shape[0]) for kv in kv_list]
        + [pair_spec(kv.shape[0], pairs) for kv in kv_list],
        out_specs=[pair_spec(row_total), pl.BlockSpec((row_total, 128), lambda i: (0, 0))],
        out_shape=[
            jax.ShapeDtypeStruct((row_total, width), jnp.bfloat16),
            jax.ShapeDtypeStruct((row_total, 128), jnp.float32),
        ],
        scratch_shapes=scratch,
        compiler_params=pltpu.CompilerParams(
            dimension_semantics=("arbitrary",), vmem_limit_bytes=VMEM_LIMIT
        ),
        cost_estimate=pl.CostEstimate(flops=1, bytes_accessed=1, transcendentals=0),
        name="attend_forward",
    )(*([scalars] if masked else []), queries, *kv_list, *kv_list)


def attend_backward(
    scalars, queries, grads, mixed, log_totals, kv_list, plan, slot_at, key_step, segs, onto=None
):
    masked = scalars is not None
    row_total, width = queries.shape
    pairs = width // (2 * HDIM)
    lse = log_totals[:, :HEADS].T.reshape(pairs, 2, row_total)
    plan = tuple(
        (q_at, q_n, kept)
        for q_at, q_n, parts in plan
        if (kept := tuple(part for part in parts if part[0] in segs))
    )
    prompt_len, slot_len = kv_list[0].shape[0], kv_list[-1].shape[0]
    kv_list = [kv_list[seg] for seg in segs]
    scratch = [pltpu.VMEM((kv.shape[0], 2 * HDIM), jnp.float32) for kv in kv_list] * 2
    if masked:
        scratch += [
            pltpu.VMEM((prompt_len if 0 in segs else 8, slot_at), jnp.float32),
            pltpu.VMEM((slot_len, slot_len) if 1 in segs else (8, 128), jnp.float32),
        ]
    area = sum(q_n * k_n for _, q_n, parts in plan for _, k_n, _ in parts)
    n_seg = len(kv_list)
    partial = masked and 1 not in segs
    given = [] if onto is None else [onto]
    outs = pl.pallas_call(
        functools.partial(bwd_kernel, plan, masked, slot_at, key_step, segs, bool(given)),
        grid=(pairs,),
        in_specs=([pl.BlockSpec(memory_space=pltpu.SMEM)] if masked else [])
        + [pair_spec(row_total)] * 3
        + [pl.BlockSpec((1, 2, row_total), lambda i: (i, 0, 0))]
        + [pair_spec(kv.shape[0]) for kv in kv_list]
        + [pair_spec(kv.shape[0], pairs) for kv in kv_list]
        + [pair_spec(row_total)] * len(given),
        out_specs=[pair_spec(row_total)] + [pair_spec(kv.shape[0]) for kv in kv_list] * 2,
        out_shape=[
            jax.ShapeDtypeStruct((row_total, width), jnp.float32 if partial else jnp.bfloat16)
        ]
        + [jax.ShapeDtypeStruct((kv.shape[0], width), jnp.bfloat16) for kv in kv_list] * 2,
        scratch_shapes=scratch,
        compiler_params=pltpu.CompilerParams(
            dimension_semantics=("arbitrary",), vmem_limit_bytes=VMEM_LIMIT
        ),
        cost_estimate=pl.CostEstimate(flops=1, bytes_accessed=1, transcendentals=0),
        name="attend_backward",
    )(*([scalars] if masked else []), queries, grads, mixed, lse, *kv_list, *kv_list, *given)
    return outs[0], outs[1 : 1 + n_seg], outs[1 + n_seg :]
def ffn_backward_kernel(
    core_ref,
    g_ref,
    h_ref,
    act_ref,
    slope_ref,
    down_ref,
    up_ref,
    down_other,
    down_mine,
    up_other,
    up_mine,
    bias_ref,
    out_ref,
    turned,
):
    step, steps = pl.program_id(0), pl.num_programs(0)
    core = core_ref[0]
    quarter = h_ref.shape[1] // 4

    @pl.when(step == 0)
    def _():
        for at, flip in ((0, 1), (1, 0)):
            for x in (0, 1):
                first = pl.multiple_of((2 * x + (core ^ flip)) * quarter, quarter)
                spot = (2 * at + x) * quarter
                turned[spot : spot + quarter, :] = h_ref[:, pl.ds(first, quarter)].T

    grad = g_ref[...]
    pre = product_nt(grad, down_ref[...]) * slope_ref[...].astype(jnp.float32)
    bias_ref[...] = jnp.sum(pre, 0, keepdims=True)
    pre = pre.astype(jnp.bfloat16)
    add = product_nt(pre, up_ref[...])

    @pl.when(step == 0)
    def _():
        out_ref[...] = add

    @pl.when(step > 0)
    def _():
        out_ref[...] += add

    up_other[...] = product(turned[: 2 * quarter, :], pre).astype(jnp.bfloat16)
    up_mine[...] = product(turned[2 * quarter :, :], pre).astype(jnp.bfloat16)
    down = product_tn(act_ref[...], grad).astype(jnp.bfloat16)

    @pl.when(step < steps // 2)
    def _():
        down_other[...] = down

    @pl.when(step >= steps // 2)
    def _():
        down_mine[...] = down


def ffn_backward(core, grad_ffn, hidden_two, act, slope, w_down, w_up, step=1024):
    rows, width = hidden_two.shape
    units = w_up.shape[1]
    steps = units // step
    inner = steps // 4
    half = steps // 2

    def unit(i, core_ref):
        other = i < half
        j = jnp.where(other, i, i - half)
        c = jnp.where(other, 1 - core_ref[0], core_ref[0])
        return ((j // inner) * 2 + c) * inner + j % inner

    whole = pl.BlockSpec((rows, width), lambda i, core_ref: (0, 0))
    block = pl.BlockSpec((rows, step), lambda i, core_ref: (0, unit(i, core_ref)))
    up_block = pl.BlockSpec((width // 2, step), lambda i, core_ref: (0, unit(i, core_ref)))
    return pl.pallas_call(
        ffn_backward_kernel,
        grid_spec=pltpu.PrefetchScalarGridSpec(
            num_scalar_prefetch=1,
            grid=(steps,),
            in_specs=[
                whole,
                whole,
                block,
                block,
                pl.BlockSpec((step, width), lambda i, core_ref: (unit(i, core_ref), 0)),
                pl.BlockSpec((width, step), lambda i, core_ref: (0, unit(i, core_ref))),
            ],
            out_specs=[
                pl.BlockSpec((step, width), lambda i, core_ref: (jnp.minimum(i, half - 1), 0)),
                pl.BlockSpec((step, width), lambda i, core_ref: (jnp.maximum(i - half, 0), 0)),
                up_block,
                up_block,
                pl.BlockSpec((1, step), lambda i, core_ref: (0, unit(i, core_ref))),
                whole,
            ],
            scratch_shapes=[pltpu.VMEM((width, rows), jnp.bfloat16)],
        ),
        out_shape=[
            jax.ShapeDtypeStruct((units // 2, width), jnp.bfloat16),
            jax.ShapeDtypeStruct((units // 2, width), jnp.bfloat16),
            jax.ShapeDtypeStruct((width // 2, units), jnp.bfloat16),
            jax.ShapeDtypeStruct((width // 2, units), jnp.bfloat16),
            jax.ShapeDtypeStruct((1, units), jnp.float32),
            jax.ShapeDtypeStruct((rows, width), jnp.float32),
        ],
        compiler_params=pltpu.CompilerParams(
            dimension_semantics=("arbitrary",), vmem_limit_bytes=VMEM_LIMIT
        ),
        cost_estimate=pl.CostEstimate(flops=1, bytes_accessed=1, transcendentals=0),
        name="ffn_backward",
    )(core, grad_ffn, hidden_two, act, slope, w_down, w_up)


def half_products_kernel(counts, has_came, core_ref, *refs):
    out_ref = refs[-1]
    came_ref = refs[-2] if has_came else None
    at = 0
    for term, count in enumerate(counts):
        pairs = [(refs[at + 2 * i], refs[at + 2 * i + 1]) for i in range(count)]
        at += 2 * count
        quarter = pairs[0][0].shape[1] // 4
        for x in (0, 1):
            rows = slice(x * quarter, (x + 1) * quarter)
            first = pl.multiple_of((2 * x + core_ref[0]) * quarter, quarter)
            total = sum(product_tn(left[:, pl.ds(first, quarter)], right[...]) for left, right in pairs)
            if has_came:
                total = total + came_ref[term, rows, :].astype(jnp.float32)
            out_ref[term, rows, :] = total.astype(jnp.bfloat16)


def half_products(core, terms, came=None):
    arrays = [matrix for pairs in terms for pair in pairs for matrix in pair]
    shape = (len(terms), arrays[0].shape[1] // 2, arrays[1].shape[1])
    given = [] if came is None else [came]
    return pl.pallas_call(
        functools.partial(
            half_products_kernel, tuple(len(pairs) for pairs in terms), came is not None
        ),
        in_specs=[pl.BlockSpec(memory_space=pltpu.SMEM)]
        + [pl.BlockSpec(memory_space=pltpu.VMEM)] * (len(arrays) + len(given)),
        out_specs=pl.BlockSpec(memory_space=pltpu.VMEM),
        out_shape=jax.ShapeDtypeStruct(shape, jnp.bfloat16),
        compiler_params=pltpu.CompilerParams(vmem_limit_bytes=VMEM_LIMIT),
        cost_estimate=pl.CostEstimate(flops=1, bytes_accessed=1, transcendentals=0),
        name="half_products",
    )(core, *arrays, *given)


def column_sum(matrix):
    return jnp.sum(matrix.astype(jnp.float32), 0)


def layer_norm(residual, gain_vec, shift_vec):
    row_mean = jnp.mean(residual, -1, keepdims=True)
    centred = residual - row_mean
    row_var = jnp.mean(centred * centred, -1, keepdims=True)
    return centred * lax.rsqrt(row_var + 1e-05) * gain_vec + shift_vec


def layer_norm_back(residual, gain_vec, grad):
    row_mean = jnp.mean(residual, -1, keepdims=True)
    centred = residual - row_mean
    row_var = jnp.mean(centred * centred, -1, keepdims=True)
    inverse = lax.rsqrt(row_var + 1e-05)
    xhat = centred * inverse
    dx = grad * gain_vec
    inner = dx - jnp.mean(dx, -1, keepdims=True) - xhat * jnp.mean(dx * xhat, -1, keepdims=True)
    return inner * inverse, jnp.sum(grad * xhat, 0), jnp.sum(grad, 0)


SWAP = ((0, 1), (1, 0))


def swap(value, axis):
    return lax.ppermute(value, axis, SWAP)


class RowSum:
    def __init__(self, part):
        self.part, self.names, self.coming = part, ["y", "z", "w"], None

    def pick(self, flip):
        axis = self.names[0]
        return lax.dynamic_index_in_dim(
            self.part, lax.axis_index(axis) ^ flip, "wzy".index(axis), keepdims=False
        )

    def operands(self):
        return [self.pick(1)]

    def launch(self, operands):
        self.coming = swap(operands[0], self.names[0])

    def add(self):
        total = self.pick(0).astype(jnp.float32) + self.coming.astype(jnp.float32)
        self.names.pop(0)
        self.part = total.astype(jnp.bfloat16) if self.names else total
        self.coming = None

    def finish(self):
        while self.names:
            if self.coming is None:
                self.launch(self.operands())
            self.add()
        return self.part


class WeightSum:
    def __init__(self, other, mine):
        self.other, self.mine = other, mine
        self.names, self.coming = ["c", "xy", "yx", "z", "w"], None

    def operands(self):
        if self.names[0] == "c":
            return [self.other]
        return [self.pick(side, 1) for side in range(len(self.sides))]

    def pick(self, side, flip):
        stage = self.names[0]
        dim = {"xy": (1, 4), "yx": (3, 1), "z": (2,), "w": (1,)}[stage][side]
        here = lax.axis_index(stage[side]) ^ flip
        return lax.dynamic_index_in_dim(self.sides[side], here, dim, keepdims=False)

    def launch(self, operands):
        self.coming = [swap(operand, axis) for operand, axis in zip(operands, self.names[0])]

    def add(self):
        f32, bf16 = jnp.float32, jnp.bfloat16
        stage, coming = self.names[0], self.coming
        if stage == "c":
            total = self.mine(coming[0])
            terms, rows, width = total.shape
            total = total.reshape(terms, 2, 2, 2, 2, rows // 16, width)
            self.sides = [total[..., : width // 2], total[..., width // 2 :]]
        else:
            self.sides = [
                self.pick(side, 0).astype(f32) + came.astype(f32)
                for side, came in enumerate(coming)
            ]
            if stage != "w":
                self.sides = [side.astype(bf16) for side in self.sides]
            if stage == "yx":
                self.sides = [jnp.concatenate(self.sides, -1)]
        self.names.pop(0)
        self.coming = None

    def finish(self):
        while self.names:
            if self.coming is None:
                self.launch(self.operands())
            self.add()
        return self.sides[0]


class Whole:
    def __init__(self, axes, parts):
        self.names, self.coming = [], None
        self.parts = [
            lax.psum_scatter(part.astype(jnp.bfloat16), axes, scatter_dimension=0, tiled=True)
            for part in parts
        ]

    def finish(self):
        return jnp.stack(self.parts).astype(jnp.float32)


def begin(value, *transfers):
    live = [t for t in transfers if t.names]
    if not live:
        return value
    value, operands = lax.optimization_barrier((value, [t.operands() for t in live]))
    for t, ready in zip(live, operands):
        t.launch(ready)
    return value


def advance(value, *transfers):
    live = [t for t in transfers if t.coming is not None]
    if not live:
        return value
    value, arrived = lax.optimization_barrier((value, [t.coming for t in live]))
    for t, coming in zip(live, arrived):
        t.coming = coming
        t.add()
    return begin(value, *live)


class Rows:
    def __init__(self, part):
        self.part, self.names, self.coming = part, (), None

    def finish(self):
        return self.part.astype(jnp.float32)


class Known:
    def __init__(self, parts):
        self.parts, self.names, self.coming = parts, (), None

    def finish(self, place):
        return self.parts


class RowGathering:
    def __init__(self, block, cuts):
        self.block, self.cuts, self.names = block, cuts, ["w", "z", "y"]
        self.coming = None

    def operands(self):
        return [self.block]

    def launch(self, operands):
        (self.block,) = operands
        self.coming = swap(self.block, self.names[0])

    def add(self):
        self.names.pop(0)
        self.block = jnp.stack([self.block, self.coming])
        self.coming = None

    def finish(self, place):
        while self.names:
            if self.coming is None:
                self.launch(self.operands())
            self.add()
        return assemble_rows(place, self.cuts, self.block)


def put_blocks(own, source, spans, outs, lead):
    shard = source.shape[-2]
    for y, z, w in itertools.product(range(2), range(2), range(2)):
        place = ((own[0] ^ w) * 2 + (own[1] ^ z)) * 2 + (own[2] ^ y)
        rows = pl.ds(pl.multiple_of(place * shard, shard), shard)
        for first, out, column, count in spans:
            outs[out][rows, column : column + count] = source[
                (*lead(y), z, w, slice(None), slice(first, first + count))
            ]


def assemble_kernel(spans, place_ref, left_own, right_own, left_came, right_came, *outs):
    own = (place_ref[2], place_ref[3], place_ref[4])
    core = pl.program_id(0)
    for which, left, right in ((0, left_own, right_own), (1, left_came, right_came)):

        @pl.when(core == which)
        def _(left=left, right=right):
            put_blocks(own, left, spans[0], outs, lambda y: (0, y))
            put_blocks(own, right, spans[1], outs, lambda y: (y, 0))


def assemble(place, spans, arrays, shapes):
    left_own, right_own, _, _ = arrays
    shard = left_own.shape[-2]

    def left_spec(which):
        def at(core, x, _):
            return (jnp.where(core == which, x, 1 - which), 0, 0, 0, 0, 0)

        return pl.BlockSpec((1, 2, 2, 2, shard, left_own.shape[-1]), at)

    def right_spec(which):
        def at(core, x, _):
            return (0, jnp.where(core == which, x, 1 - which), 0, 0, 0, 0)

        return pl.BlockSpec((2, 1, 2, 2, shard, right_own.shape[-1]), at)

    def out_at(core, x, place_ref):
        return ((place_ref[0] ^ x) * 2 + (place_ref[1] ^ core), 0)

    return pl.pallas_call(
        functools.partial(assemble_kernel, spans),
        grid_spec=pltpu.PrefetchScalarGridSpec(
            num_scalar_prefetch=1,
            grid=(2, 2),
            in_specs=[left_spec(0), right_spec(0), left_spec(1), right_spec(1)],
            out_specs=[pl.BlockSpec((8 * shard, shape[1]), out_at) for shape in shapes],
        ),
        out_shape=[jax.ShapeDtypeStruct(shape, jnp.bfloat16) for shape in shapes],
        compiler_params=pltpu.CompilerParams(
            dimension_semantics=("arbitrary", "arbitrary"), vmem_limit_bytes=VMEM_LIMIT
        ),
        cost_estimate=pl.CostEstimate(
            flops=0, transcendentals=0, bytes_accessed=sum(4 * array.size for array in arrays)
        ),
        name="assemble",
    )(place, *arrays)


def assemble_rows_kernel(cuts, place_ref, source, *outs):
    own = (place_ref[2], place_ref[3], place_ref[4])
    for out, (first, count) in zip(outs, cuts):
        for y, z, w in itertools.product(range(2), range(2), range(2)):
            block = ((own[0] ^ w) * 2 + (own[1] ^ z)) * 2 + (own[2] ^ y)
            rows = pl.ds(pl.multiple_of(block * count, count), count)
            out[rows, :] = source[y, z, w, first : first + count, :]


def assemble_rows(place, cuts, gathered):
    width = gathered.shape[-1]
    return pl.pallas_call(
        functools.partial(assemble_rows_kernel, cuts),
        in_specs=[pl.BlockSpec(memory_space=pltpu.SMEM), pl.BlockSpec(memory_space=pltpu.VMEM)],
        out_specs=[pl.BlockSpec(memory_space=pltpu.VMEM) for _ in cuts],
        out_shape=[jax.ShapeDtypeStruct((8 * count, width), jnp.bfloat16) for _, count in cuts],
        compiler_params=pltpu.CompilerParams(vmem_limit_bytes=VMEM_LIMIT),
        cost_estimate=pl.CostEstimate(
            flops=0, transcendentals=0, bytes_accessed=4 * gathered.size
        ),
        name="assemble_rows",
    )(place, gathered)


class Gathering:
    def __init__(self, block, cut, spans, shapes):
        self.sides, self.cut = [block], cut
        self.spans, self.shapes = spans, shapes
        self.names, self.coming = ["w", "z", "yx", "xy", "cc"], None

    def operands(self):
        return self.sides

    def launch(self, operands):
        self.sides = operands
        self.coming = [swap(side, axis) for side, axis in zip(operands, self.names[0])]

    def add(self):
        stage = self.names.pop(0)
        coming, self.coming = self.coming, None
        if stage == "cc":
            self.arrived = coming
        elif stage == "z":
            pair = [self.sides[0], coming[0]]
            self.sides = [
                jnp.stack([block[..., : self.cut] for block in pair]),
                jnp.stack([block[..., self.cut :] for block in pair]),
            ]
        else:
            self.sides = [jnp.stack(pair) for pair in zip(self.sides, coming)]

    def finish(self, place):
        while self.names:
            if self.coming is None:
                self.launch(self.operands())
            self.add()
        return assemble(place, self.spans, [*self.sides, *self.arrived], self.shapes)


class Links:
    def __init__(self, mesh):
        self.fast = dict(mesh.shape) == {"fsdp": 4, "ctx": 8}
        if self.fast:
            self.mesh = Mesh(mesh.devices.reshape(2, 2, 2, 2, 2), ("x", "c", "w", "z", "y"))
            self.rows, self.ctx = ("x", "c"), ("w", "z", "y")
        else:
            self.mesh, self.rows, self.ctx = mesh, ("fsdp",), ("ctx",)
        self.every = self.rows + self.ctx

    def place(self):
        axes = self.every if self.fast else ()
        return jnp.stack([lax.axis_index(axis).astype(jnp.int32) for axis in axes or self.rows])

    def gather(self, weights, cut):
        if not self.fast:
            return Known([lax.all_gather(w, self.every, axis=0, tiled=True) for w in weights])
        shapes = tuple((32 * w.shape[0], w.shape[1]) for w in weights)
        block = weights[0] if len(weights) == 1 else jnp.concatenate(weights, 1)
        first, left, right = 0, [], []
        for out, weight in enumerate(weights):
            count = weight.shape[1]
            low = min(max(cut - first, 0), count)
            if low:
                left.append((first, out, 0, low))
            if low < count:
                right.append((first + low - cut, out, low, count - low))
            first += count
        return Gathering(block, cut, (tuple(left), tuple(right)), shapes)

    def gather_once(self, weights):
        return lax.all_gather(jnp.concatenate(weights, 1), self.every, axis=0, tiled=True)

    def gather_rows(self, parts):
        if not self.fast:
            return Known([lax.all_gather(part, self.ctx, axis=0, tiled=True) for part in parts])
        cuts, first = [], 0
        for part in parts:
            cuts.append((first, part.shape[0]))
            first += part.shape[0]
        return RowGathering(jnp.concatenate(parts, 0), tuple(cuts))

    def weight_sum(self, terms):
        if not self.fast:
            return Whole(
                self.every,
                [sum(product_tn(left, right) for left, right in pairs) for pairs in terms],
            )
        core = lax.axis_index("c").astype(jnp.int32).reshape(1)
        return WeightSum(
            half_products(1 - core, terms), lambda came: half_products(core, terms, came)
        )

    def row_sum(self, part):
        part = part.astype(jnp.bfloat16)
        if not self.fast:
            return Rows(lax.psum_scatter(part, self.ctx, scatter_dimension=0, tiled=True))
        return RowSum(part.reshape(2, 2, 2, part.shape[0] // 8, part.shape[1]))


def body(
    links,
    prompt_in,
    cont_in,
    encoder,
    prompt_start,
    cont_start,
    self_proj,
    self_out,
    cross_query,
    cross_kv,
    cross_out,
    up_proj,
    down_proj,
    vec_bias,
    up_bias,
    ln_gain,
    ln_bias,
    prompt_cot,
    cont_cot,
):
    f32, bf16 = jnp.float32, jnp.bfloat16
    shard, width = self_out.shape
    prompt_rows, slot_len = prompt_in.shape[1], cont_in.shape[2]
    block_index = lax.axis_index(links.ctx)
    ctx_count = lax.axis_size(links.ctx)
    prompt_len = prompt_rows * ctx_count
    enc_rows = encoder.shape[1]
    hidden = up_bias.shape[0] // shard
    scale = HDIM ** (-0.5)

    small = jnp.concatenate(
        [vec_bias.T, ln_gain.T, ln_bias.T, up_bias.reshape(hidden, shard).T], 1
    )
    small = jnp.pad(small, ((0, 0), (0, 128 - small.shape[1])))
    place = links.place()
    rows_in = links.gather_rows([prompt_in[0], encoder[0]])
    first = links.gather([self_proj, small], 13 * 128)
    second = links.gather([self_out, cross_query, cross_kv, cross_out], 20 * 128)
    up = links.gather([up_proj], 16 * 128)
    tokens = jnp.concatenate([prompt_in[0], cont_in[0, 0]], 0)
    tokens = begin(tokens, first, rows_in)
    tokens = advance(tokens, first)
    tokens = advance(tokens, first, rows_in)
    tokens = begin(tokens, second)
    tokens = advance(tokens, first)
    tokens = advance(tokens, rows_in, second)
    tokens = advance(tokens, first)
    tokens, down_proj = begin((tokens, down_proj), up)
    w_down = lax.all_gather(down_proj, links.every, axis=0, tiled=True)
    tokens = advance(tokens, first)
    self_w, small = first.finish(place)
    w_q, w_kv = self_w[:, :width], self_w[:, width:]
    small = small.astype(f32).T
    biases, gains, shifts = small[:7], small[7:10], small[10:13]
    hidden_bias = (
        small[13 : 13 + hidden]
        .reshape(hidden, width // shard, shard)
        .transpose(1, 0, 2)
        .reshape(hidden * width)
    )

    every_begin = cont_start[0]
    own_begin = lax.dynamic_index_in_dim(every_begin, block_index, 0, keepdims=False)
    scalars = jnp.stack([prompt_start[0], own_begin, block_index.astype(jnp.int32)])
    cont_rows = tokens[prompt_rows:]
    row_total = tokens.shape[0]
    row_spot = jnp.arange(row_total, dtype=jnp.int32)
    valid_rows = jnp.where(
        row_spot < prompt_rows,
        block_index * prompt_rows + row_spot >= prompt_start[0],
        row_spot - prompt_rows >= own_begin,
    ).astype(f32)[:, None]
    valid_count = (prompt_len - prompt_start[0] + jnp.sum(slot_len - every_begin)).astype(f32)

    kv_bias = jnp.concatenate([jnp.zeros((width,), f32), biases[1]])
    queries = ((product(tokens, w_q) + biases[0]) * scale).astype(bf16)
    cont_kv = (product(cont_rows, w_kv) + kv_bias).astype(bf16)
    (queries, cont_kv) = advance((queries, cont_kv), second, up)
    queries = advance(queries, rows_in)
    prompt_all, enc_all = rows_in.finish(place)
    prompt_kv = (product(prompt_all, w_kv) + kv_bias).astype(bf16)
    plan = self_plan(prompt_rows, prompt_len, slot_len)
    prompt_kv = advance(prompt_kv, second)
    attn, self_log = attend_forward(scalars, queries, [prompt_kv, cont_kv], plan, prompt_rows)
    attn = advance(attn, second, up)
    attn = advance(attn, second)
    w_so, w_cq, w_ckv, w_co = second.finish(place)
    branch_self = product(attn, w_so) + biases[2]
    resid_one = tokens.astype(f32) + branch_self
    hidden_one = layer_norm(resid_one, gains[0], shifts[0]).astype(bf16)

    enc_bias = jnp.concatenate([jnp.zeros((width,), f32), biases[4]])
    enc_kv = (product(enc_all, w_ckv) + enc_bias).astype(bf16)
    cross_queries = ((product(hidden_one, w_cq) + biases[3]) * scale).astype(bf16)
    enc_len = enc_all.shape[0]
    cross_queries = advance(cross_queries, up)
    cross_attn, cross_log = attend_forward(
        None, cross_queries, [enc_kv], cross_plan(row_total, enc_len, 320), 0
    )
    cross_attn = advance(cross_attn, up)
    (w_up,) = up.finish(place)
    branch_cross = product(cross_attn, w_co) + biases[5]
    resid_two = hidden_one.astype(f32) + branch_cross
    hidden_two = layer_norm(resid_two, gains[1], shifts[1]).astype(bf16)

    pre_act = product(hidden_two, w_up) + hidden_bias
    half = 0.5 * (1.0 + lax.erf(pre_act * (0.5**0.5)))
    act = (pre_act * half).astype(bf16)
    slope = (half + pre_act * jnp.exp(-0.5 * pre_act * pre_act) * 0.3989422804014327).astype(bf16)
    branch_ffn = product(act, w_down) + biases[6]
    resid_three = hidden_two.astype(f32) + branch_ffn
    output = layer_norm(resid_three, gains[2], shifts[2]).astype(bf16)

    members = (tokens, branch_self, hidden_one, branch_cross, hidden_two, branch_ffn)
    squares = jnp.stack(
        [jnp.sum(valid_rows * jnp.square(member.astype(f32)), 0) for member in members]
    )
    grad_out = jnp.concatenate([prompt_cot[0], cont_cot[0, 0]], 0).astype(f32)
    grad_three, gain_three, shift_three = layer_norm_back(resid_three, gains[2], grad_out)
    grad_ffn = grad_three.astype(bf16)
    half_width = width // 2
    if links.fast:
        core = lax.axis_index("c").astype(jnp.int32).reshape(1)
        down_other, down_mine, up_other, up_mine, up_bias_part, back_ffn = ffn_backward(
            core, grad_ffn, hidden_two, act, slope, w_down, w_up
        )

        def add_to(mine):
            return lambda came: (mine.astype(f32) + came[0].astype(f32)).astype(bf16)[None]

        down_sum = WeightSum(down_other[None], add_to(down_mine))
        up_sum = WeightSum(up_other[None], add_to(up_mine))
    else:
        grad_pre = (product_nt(grad_ffn, w_down) * slope.astype(f32)).astype(bf16)
        down_sum = links.weight_sum([[(act, grad_ffn)]])
        up_sum = links.weight_sum([[(hidden_two, grad_pre)]])
        up_bias_part = column_sum(grad_pre)
        back_ffn = product_nt(grad_pre, w_up)
    back_ffn = begin(back_ffn, down_sum, up_sum)
    grad_hidden_two = grad_three + back_ffn
    grad_two, gain_two, shift_two = layer_norm_back(resid_two, gains[1], grad_hidden_two)
    grad_cross = grad_two.astype(bf16)
    grad_cattn = product_nt(grad_cross, w_co).astype(bf16)
    grad_cattn = advance(grad_cattn, down_sum)
    cross_gq, cross_gk, cross_gv = attend_backward(
        None,
        cross_queries,
        grad_cattn,
        cross_attn,
        cross_log,
        [enc_kv],
        cross_plan(row_total, enc_len, 384),
        0,
        512,
        (0,),
    )
    cross_gq = advance(cross_gq, down_sum, up_sum)
    grad_cq = (cross_gq.astype(f32) * scale).astype(bf16)
    enc_back = product_nt(cross_gk[0], w_ckv[:, :width]) + product_nt(
        cross_gv[0], w_ckv[:, width:]
    )
    enc_sum = links.row_sum(enc_back)
    grad_cq = begin(grad_cq, enc_sum)
    grad_hidden_one = grad_two + product_nt(grad_cq, w_cq)
    grad_one, gain_one, shift_one = layer_norm_back(resid_one, gains[0], grad_hidden_one)
    grad_self = grad_one.astype(bf16)
    mid_sum = links.weight_sum(
        [
            [(cross_attn, grad_cross)],
            [(hidden_one, grad_cq)],
            [(attn, grad_self)],
            [(enc_all, cross_gk[0])],
            [(enc_all, cross_gv[0])],
        ]
    )
    grad_self = begin(grad_self, mid_sum)
    grad_attn = product_nt(grad_self, w_so).astype(bf16)
    small_part = jnp.concatenate(
        [
            squares,
            jnp.stack(
                [
                    column_sum(grad_self),
                    column_sum(grad_cq),
                    column_sum(cross_gv[0]),
                    column_sum(grad_cross),
                    column_sum(grad_ffn),
                    gain_one,
                    gain_two,
                    gain_three,
                    shift_one,
                    shift_two,
                    shift_three,
                ]
            ),
            up_bias_part.reshape(width // shard, hidden, shard)
            .transpose(1, 0, 2)
            .reshape(hidden, width),
        ],
        0,
    )
    grad_attn, small_part = lax.optimization_barrier((grad_attn, small_part))
    grad_attn = advance(grad_attn, down_sum, up_sum)
    grad_attn = advance(grad_attn, mid_sum)
    self_args = (queries, grad_attn, attn, self_log, [prompt_kv, cont_kv], plan, prompt_rows)
    part_gq, prompt_gk, prompt_gv = attend_backward(scalars, *self_args, 1024, (0,))
    prompt_gk, prompt_gv = prompt_gk[0], prompt_gv[0]
    w_k, w_v = w_kv[:, :width], w_kv[:, width:]
    part_gq = advance(part_gq, up_sum, mid_sum, enc_sum, down_sum)
    prompt_sum = links.row_sum(product_nt(prompt_gk, w_k) + product_nt(prompt_gv, w_v))
    part_gq = begin(part_gq, prompt_sum)
    self_gq, cont_gk, cont_gv = attend_backward(scalars, *self_args, 512, (1,), part_gq)
    cont_gk, cont_gv = cont_gk[0], cont_gv[0]
    self_gq = advance(self_gq, down_sum, up_sum, mid_sum, prompt_sum, enc_sum)
    grad_q = (self_gq.astype(f32) * scale).astype(bf16)

    last_part = jnp.stack([column_sum(grad_q), column_sum(prompt_gv) + column_sum(cont_gv)])
    small_part = jnp.concatenate(
        [small_part, last_part, jnp.zeros((32 - small_part.shape[0] - 2, width), f32)], 0
    )
    small_all = lax.all_gather(small_part, links.every, axis=0, tiled=True)
    self_sum = links.weight_sum(
        [
            [(tokens, grad_q)],
            [(prompt_all, prompt_gk), (cont_rows, cont_gk)],
            [(prompt_all, prompt_gv), (cont_rows, cont_gv)],
        ]
    )
    grad_q = begin(grad_q, self_sum)
    input_grad = grad_one + product_nt(grad_q, w_q)
    cont_grad = input_grad[prompt_rows:] + product_nt(cont_gk, w_k) + product_nt(cont_gv, w_v)
    cont_grad = advance(cont_grad, self_sum)
    cont_grad = advance(cont_grad, mid_sum, prompt_sum)
    cont_grad = advance(cont_grad, self_sum, up_sum)
    cont_grad = advance(cont_grad, self_sum)
    cont_grad = advance(cont_grad, self_sum, mid_sum, prompt_sum, enc_sum)[None, None]
    prompt_grad = (input_grad[:prompt_rows] + prompt_sum.finish())[None]
    encoder_grad = enc_sum.finish()[None]
    up_total, down_total = up_sum.finish()[0], down_sum.finish()[0]
    co_total, cq_total, so_total, ck_total, cv_total = mid_sum.finish()
    ckv_total = jnp.concatenate([ck_total, cv_total], 1)
    sin_total = jnp.concatenate([*self_sum.finish()], 1)
    small_all = small_all.reshape(-1, ctx_count, 32, width)
    group = lax.axis_index(links.rows)
    squares = jnp.sum(lax.dynamic_index_in_dim(small_all, group, 0, keepdims=False)[:, :6], (0, 2))
    statistics = (squares / (valid_count * width))[None]
    at = lax.axis_index(links.every) * shard
    sums = jnp.sum(lax.dynamic_slice_in_dim(small_all, at, shard, 3), (0, 1))
    bias_total = jnp.concatenate([sums[21:23], sums[6:11]])
    gain_total, shift_total = sums[11:14], sums[14:17]
    up_bias_total = sums[17 : 17 + hidden].reshape(hidden * shard)
    return (
        output[:prompt_rows][None],
        output[prompt_rows:][None, None],
        prompt_grad,
        cont_grad,
        encoder_grad,
        sin_total,
        so_total,
        cq_total,
        ckv_total,
        co_total,
        up_total,
        down_total,
        bias_total,
        up_bias_total,
        gain_total,
        shift_total,
        statistics,
    )


def solution(mesh):
    links = Links(mesh)
    fs, ctx, every = links.rows, links.ctx, links.every
    group = P(fs, ctx, None)
    slots = P(fs, ctx, None, None)
    weight = P(every, None)
    vectors = P(None, every)
    return jax.shard_map(
        functools.partial(body, links),
        mesh=links.mesh,
        in_specs=(group, slots, group, P(fs), P(fs, None))
        + (weight,) * 7
        + (vectors, P(every), vectors, vectors, group, slots),
        out_specs=(group, slots, group, slots, group)
        + (weight,) * 7
        + (vectors, P(every), vectors, vectors, P(fs, None)),
        check_vma=False,
    )
```

```python
import functools
import itertools

import jax
import jax.numpy as jnp
from jax import lax
from jax.experimental import pallas as pl
from jax.experimental.pallas import tpu as pltpu
from jax.sharding import Mesh
from jax.sharding import PartitionSpec as P

HEADS = 16
HDIM = 64
MASKED = -1e30


def product(first_mat, second_mat):
    return jnp.dot(first_mat, second_mat, preferred_element_type=jnp.float32)


def product_tn(first_mat, second_mat):
    return lax.dot_general(
        first_mat, second_mat, (((0,), (0,)), ((), ())), preferred_element_type=jnp.float32
    )


def product_nt(first_mat, second_mat):
    return lax.dot_general(
        first_mat, second_mat, (((1,), (1,)), ((), ())), preferred_element_type=jnp.float32
    )


def bias_fill(sc_ref, prompt_bias, own_bias, flip, segs=(0, 1)):
    begin, cont_begin, block = sc_ref[0], sc_ref[1], sc_ref[2]
    q_dim, k_dim = (1, 0) if flip else (0, 1)
    if 0 in segs:
        shape = prompt_bias.shape
        rows = shape[q_dim]
        spot = lax.broadcasted_iota(jnp.int32, shape, q_dim) + block * rows
        key = lax.broadcasted_iota(jnp.int32, shape, k_dim)
        seen = (key <= spot) & ((key >= begin) | (key == spot))
        prompt_bias[...] = jnp.where(seen, 0.0, MASKED)
    if 1 in segs:
        shape = own_bias.shape
        spot = lax.broadcasted_iota(jnp.int32, shape, q_dim)
        key = lax.broadcasted_iota(jnp.int32, shape, k_dim)
        seen = (key <= spot) & ((key >= cont_begin) | (key == spot))
        own_bias[...] = jnp.where(seen, 0.0, MASKED)


def self_plan(prompt_rows, prompt_len, slot_len):
    step = slot_len // 2
    return (
        (0, prompt_rows, ((0, prompt_len, "prompt"),)),
        (prompt_rows, step, ((0, prompt_len, "start"), (1, step, "own"))),
        (prompt_rows + step, slot_len - step, ((0, prompt_len, "start"), (1, slot_len, "own"))),
    )


def cross_plan(row_total, key_total, step):
    return tuple(
        (at, min(step, row_total - at), ((0, key_total, None),)) for at in range(0, row_total, step)
    )


def head_lanes(head):
    lane = lax.broadcasted_iota(jnp.int32, (1, 2 * HDIM), 1)
    return (lane >= head * HDIM) & (lane < (head + 1) * HDIM)


def only(block, lanes):
    return jnp.where(lanes, block, jnp.zeros_like(block))


def fwd_kernel(plan, masked, slot_at, *refs):
    n_seg = 2 if masked else 1
    if masked:
        sc_ref, refs = refs[0], refs[1:]
    q_ref = refs[0]
    k_refs, v_refs = refs[1 : 1 + n_seg], refs[1 + n_seg : 1 + 2 * n_seg]
    o_ref, lse_ref = refs[1 + 2 * n_seg : 3 + 2 * n_seg]
    pair = pl.program_id(0)
    if masked:
        prompt_bias, own_bias = refs[3 + 2 * n_seg :]

        @pl.when(pair == 0)
        def _():
            bias_fill(sc_ref, prompt_bias, own_bias, False)

    out_lane = lax.broadcasted_iota(jnp.int32, (1, 128), 1)
    for q_at, q_n, parts in plan:
        rows = slice(q_at, q_at + q_n)
        q_blk = q_ref[rows, :]
        mixed_pair = None
        for head in (0, 1):
            lanes = head_lanes(head)
            q_one = only(q_blk, lanes)
            scores = []
            for seg, k_n, kind in parts:
                part = product_nt(q_one, k_refs[seg][:k_n, :])
                if kind == "prompt":
                    part = part + prompt_bias[...]
                elif kind == "own":
                    at = q_at - slot_at
                    part = part + own_bias[at : at + q_n, :k_n]
                elif kind == "start":
                    key = lax.broadcasted_iota(jnp.int32, (1, 128), 1)
                    first = jnp.where(key >= sc_ref[0], part[:, :128], MASKED)
                    part = jnp.concatenate([first, part[:, 128:]], 1)
                scores.append(part)
            row_max = functools.reduce(
                jnp.maximum, [jnp.max(part, 1, keepdims=True) for part in scores]
            )
            totals, mixed = 0.0, 0.0
            for part, (seg, k_n, _) in zip(scores, parts):
                shifted = jnp.exp(part - row_max)
                totals = totals + jnp.sum(shifted, 1, keepdims=True)
                mixed = mixed + product(shifted.astype(jnp.bfloat16), v_refs[seg][:k_n, :])
            mixed = mixed / totals
            mixed_pair = mixed if head == 0 else jnp.where(lanes, mixed, mixed_pair)
            lse = row_max + jnp.log(totals)
            lse_ref[rows, :] = jnp.where(out_lane == 2 * pair + head, lse, lse_ref[rows, :])
        o_ref[rows, :] = mixed_pair.astype(jnp.bfloat16)


def accumulate(total_ref, keys, done, part):
    known = min(max(done - keys.start, 0), keys.stop - keys.start)
    if known:
        total_ref[keys.start : keys.start + known, :] += part[:known]
    if known < keys.stop - keys.start:
        total_ref[keys.start + known : keys.stop, :] = part[known:]


def bwd_kernel(plan, masked, slot_at, key_step, segs, onto, *refs):
    n_seg = len(segs)
    if masked:
        sc_ref, refs = refs[0], refs[1:]
    q_ref, g_ref, o_ref, lse_ref = refs[:4]
    k_refs, v_refs = refs[4 : 4 + n_seg], refs[4 + n_seg : 4 + 2 * n_seg]
    outs = refs[4 + 2 * n_seg :]
    if onto:
        dq_in, outs = outs[0], outs[1:]
        dq_in_rows = slice(0, plan[0][0])
        outs[0][dq_in_rows, :] = dq_in[dq_in_rows, :].astype(outs[0].dtype)
    dq_ref, dk_refs, dv_refs = outs[0], outs[1 : 1 + n_seg], outs[1 + n_seg : 1 + 2 * n_seg]
    scratch = outs[1 + 2 * n_seg :]
    dk_acc, dv_acc = scratch[:n_seg], scratch[n_seg : 2 * n_seg]
    pair = pl.program_id(0)
    if masked:
        prompt_bias, own_bias = scratch[2 * n_seg :]

        @pl.when(pair == 0)
        def _():
            bias_fill(sc_ref, prompt_bias, own_bias, True, segs)

    done = [0] * n_seg
    picks = jnp.concatenate(
        [only(jnp.ones((1, 2 * HDIM), jnp.float32), head_lanes(h)) for h in (0, 1)]
        + [jnp.zeros((6, 2 * HDIM), jnp.float32)],
        0,
    )
    for q_at, q_n, parts in plan:
        rows = slice(q_at, q_at + q_n)
        q_blk, g_blk = q_ref[rows, :], g_ref[rows, :]
        inner = lax.dot_general(
            picks,
            g_blk.astype(jnp.float32) * o_ref[rows, :].astype(jnp.float32),
            (((1,), (1,)), ((), ())),
            precision=lax.Precision.HIGHEST,
            preferred_element_type=jnp.float32,
        )
        dq = dq_in[rows, :] if onto else 0.0
        for head in (0, 1):
            lanes = head_lanes(head)
            q_one, g_one = only(q_blk, lanes), only(g_blk, lanes)
            lse = lse_ref[0, head : head + 1, rows]
            row_inner = inner[head : head + 1, :]
            for which, k_n, kind in parts:
                seg = segs.index(which)
                for at in range(0, k_n, key_step):
                    keys = slice(at, min(at + key_step, k_n))
                    k_one = only(k_refs[seg][keys, :], lanes)
                    scores = product_nt(k_one, q_blk)
                    if kind == "prompt":
                        scores = scores + prompt_bias[keys, :]
                    elif kind == "own":
                        q_off = q_at - slot_at
                        scores = scores + own_bias[keys, q_off : q_off + q_n]
                    elif kind == "start" and at == 0:
                        key = lax.broadcasted_iota(jnp.int32, (128, 1), 0)
                        first = jnp.where(key >= sc_ref[0], scores[:128, :], MASKED)
                        scores = jnp.concatenate([first, scores[128:, :]], 0)
                    probs = jnp.exp(scores - lse)
                    grad_probs = product_nt(v_refs[seg][keys, :], g_one)
                    grad_scores = (probs * (grad_probs - row_inner)).astype(jnp.bfloat16)
                    add_v = product(probs.astype(jnp.bfloat16), g_one)
                    add_k = product(grad_scores, q_one)
                    accumulate(dv_acc[seg], keys, done[seg], add_v)
                    accumulate(dk_acc[seg], keys, done[seg], add_k)
                    dq = dq + product_tn(grad_scores, k_one)
                done[seg] = max(done[seg], k_n)
        dq_ref[rows, :] = dq.astype(dq_ref.dtype)
    for seg in range(n_seg):
        dk_refs[seg][...] = dk_acc[seg][...].astype(jnp.bfloat16)
        dv_refs[seg][...] = dv_acc[seg][...].astype(jnp.bfloat16)


VMEM_LIMIT = 48 * 1024 * 1024


def pair_spec(rows, shift=0):
    return pl.BlockSpec((rows, 2 * HDIM), lambda i: (0, i + shift))


def attend_forward(scalars, queries, kv_list, plan, slot_at):
    masked = scalars is not None
    row_total, width = queries.shape
    pairs = width // (2 * HDIM)
    scratch = []
    if masked:
        prompt_len, slot_len = kv_list[0].shape[0], kv_list[1].shape[0]
        scratch = [
            pltpu.VMEM((slot_at, prompt_len), jnp.float32),
            pltpu.VMEM((slot_len, slot_len), jnp.float32),
        ]
    area = sum(q_n * k_n for _, q_n, parts in plan for _, k_n, _ in parts)
    return pl.pallas_call(
        functools.partial(fwd_kernel, plan, masked, slot_at),
        grid=(pairs,),
        in_specs=([pl.BlockSpec(memory_space=pltpu.SMEM)] if masked else [])
        + [pair_spec(row_total)]
        + [pair_spec(kv.shape[0]) for kv in kv_list]
        + [pair_spec(kv.shape[0], pairs) for kv in kv_list],
        out_specs=[pair_spec(row_total), pl.BlockSpec((row_total, 128), lambda i: (0, 0))],
        out_shape=[
            jax.ShapeDtypeStruct((row_total, width), jnp.bfloat16),
            jax.ShapeDtypeStruct((row_total, 128), jnp.float32),
        ],
        scratch_shapes=scratch,
        compiler_params=pltpu.CompilerParams(
            dimension_semantics=("arbitrary",), vmem_limit_bytes=VMEM_LIMIT
        ),
        cost_estimate=pl.CostEstimate(flops=1, bytes_accessed=1, transcendentals=0),
        name="attend_forward",
    )(*([scalars] if masked else []), queries, *kv_list, *kv_list)


def attend_backward(
    scalars, queries, grads, mixed, log_totals, kv_list, plan, slot_at, key_step, segs, onto=None
):
    masked = scalars is not None
    row_total, width = queries.shape
    pairs = width // (2 * HDIM)
    lse = log_totals[:, :HEADS].T.reshape(pairs, 2, row_total)
    plan = tuple(
        (q_at, q_n, kept)
        for q_at, q_n, parts in plan
        if (kept := tuple(part for part in parts if part[0] in segs))
    )
    prompt_len, slot_len = kv_list[0].shape[0], kv_list[-1].shape[0]
    kv_list = [kv_list[seg] for seg in segs]
    scratch = [pltpu.VMEM((kv.shape[0], 2 * HDIM), jnp.float32) for kv in kv_list] * 2
    if masked:
        scratch += [
            pltpu.VMEM((prompt_len if 0 in segs else 8, slot_at), jnp.float32),
            pltpu.VMEM((slot_len, slot_len) if 1 in segs else (8, 128), jnp.float32),
        ]
    area = sum(q_n * k_n for _, q_n, parts in plan for _, k_n, _ in parts)
    n_seg = len(kv_list)
    partial = masked and 1 not in segs
    given = [] if onto is None else [onto]
    outs = pl.pallas_call(
        functools.partial(bwd_kernel, plan, masked, slot_at, key_step, segs, bool(given)),
        grid=(pairs,),
        in_specs=([pl.BlockSpec(memory_space=pltpu.SMEM)] if masked else [])
        + [pair_spec(row_total)] * 3
        + [pl.BlockSpec((1, 2, row_total), lambda i: (i, 0, 0))]
        + [pair_spec(kv.shape[0]) for kv in kv_list]
        + [pair_spec(kv.shape[0], pairs) for kv in kv_list]
        + [pair_spec(row_total)] * len(given),
        out_specs=[pair_spec(row_total)] + [pair_spec(kv.shape[0]) for kv in kv_list] * 2,
        out_shape=[
            jax.ShapeDtypeStruct((row_total, width), jnp.float32 if partial else jnp.bfloat16)
        ]
        + [jax.ShapeDtypeStruct((kv.shape[0], width), jnp.bfloat16) for kv in kv_list] * 2,
        scratch_shapes=scratch,
        compiler_params=pltpu.CompilerParams(
            dimension_semantics=("arbitrary",), vmem_limit_bytes=VMEM_LIMIT
        ),
        cost_estimate=pl.CostEstimate(flops=1, bytes_accessed=1, transcendentals=0),
        name="attend_backward",
    )(*([scalars] if masked else []), queries, grads, mixed, lse, *kv_list, *kv_list, *given)
    return outs[0], outs[1 : 1 + n_seg], outs[1 + n_seg :]
def ffn_forward_kernel(h_ref, up_ref, bias_ref, down_ref, act_ref, slope_ref, out_ref):
    step = pl.program_id(0)
    rows = h_ref.shape[0]
    half = rows // 2
    for at in (0, half):
        part = slice(at, at + half)
        pre = product(h_ref[part, :], up_ref[...]) + bias_ref[...]
        cdf = 0.5 * (1.0 + lax.erf(pre * (0.5**0.5)))
        act = (pre * cdf).astype(jnp.bfloat16)
        act_ref[part, :] = act
        slope = cdf + pre * jnp.exp(-0.5 * pre * pre) * 0.3989422804014327
        slope_ref[part, :] = slope.astype(jnp.bfloat16)
        add = product(act, down_ref[...])

        @pl.when(step == 0)
        def _(part=part, add=add):
            out_ref[part, :] = add

        @pl.when(step > 0)
        def _(part=part, add=add):
            out_ref[part, :] += add


def ffn_forward(hidden_two, w_up, up_bias, w_down, step=1024):
    rows, width = hidden_two.shape
    units = w_up.shape[1]
    whole = pl.BlockSpec((rows, width), lambda i: (0, 0))
    block = pl.BlockSpec((rows, step), lambda i: (0, i))
    return pl.pallas_call(
        ffn_forward_kernel,
        grid=(units // step,),
        in_specs=[
            whole,
            pl.BlockSpec((width, step), lambda i: (0, i)),
            pl.BlockSpec((1, step), lambda i: (0, i)),
            pl.BlockSpec((step, width), lambda i: (i, 0)),
        ],
        out_specs=[block, block, whole],
        out_shape=[
            jax.ShapeDtypeStruct((rows, units), jnp.bfloat16),
            jax.ShapeDtypeStruct((rows, units), jnp.bfloat16),
            jax.ShapeDtypeStruct((rows, width), jnp.float32),
        ],
        compiler_params=pltpu.CompilerParams(
            dimension_semantics=("arbitrary",), vmem_limit_bytes=VMEM_LIMIT
        ),
        cost_estimate=pl.CostEstimate(flops=1, bytes_accessed=1, transcendentals=0),
        name="ffn_forward",
    )(hidden_two, w_up, up_bias.reshape(1, units), w_down)


def ffn_backward_kernel(
    core_ref,
    g_ref,
    h_ref,
    act_ref,
    slope_ref,
    down_ref,
    up_ref,
    down_other,
    down_mine,
    up_other,
    up_mine,
    bias_ref,
    out_ref,
    turned,
):
    step, steps = pl.program_id(0), pl.num_programs(0)
    core = core_ref[0]
    quarter = h_ref.shape[1] // 4

    @pl.when(step == 0)
    def _():
        for at, flip in ((0, 1), (1, 0)):
            for x in (0, 1):
                first = pl.multiple_of((2 * x + (core ^ flip)) * quarter, quarter)
                spot = (2 * at + x) * quarter
                turned[spot : spot + quarter, :] = h_ref[:, pl.ds(first, quarter)].T

    grad = g_ref[...]
    pre = product_nt(grad, down_ref[...]) * slope_ref[...].astype(jnp.float32)
    bias_ref[...] = jnp.sum(pre, 0, keepdims=True)
    pre = pre.astype(jnp.bfloat16)
    add = product_nt(pre, up_ref[...])

    @pl.when(step == 0)
    def _():
        out_ref[...] = add

    @pl.when(step > 0)
    def _():
        out_ref[...] += add

    up = product(turned[...], pre).astype(jnp.bfloat16)
    up_other[...] = up[: 2 * quarter]
    up_mine[...] = up[2 * quarter :]
    down = product_tn(act_ref[...], grad).astype(jnp.bfloat16)

    @pl.when(step < steps // 2)
    def _():
        down_other[...] = down

    @pl.when(step >= steps // 2)
    def _():
        down_mine[...] = down


def ffn_backward(core, grad_ffn, hidden_two, act, slope, w_down, w_up, step=1024):
    rows, width = hidden_two.shape
    units = w_up.shape[1]
    steps = units // step
    inner = steps // 4
    half = steps // 2

    def unit(i, core_ref):
        other = i < half
        j = jnp.where(other, i, i - half)
        c = jnp.where(other, 1 - core_ref[0], core_ref[0])
        return ((j // inner) * 2 + c) * inner + j % inner

    whole = pl.BlockSpec((rows, width), lambda i, core_ref: (0, 0))
    block = pl.BlockSpec((rows, step), lambda i, core_ref: (0, unit(i, core_ref)))
    up_block = pl.BlockSpec((width // 2, step), lambda i, core_ref: (0, unit(i, core_ref)))
    return pl.pallas_call(
        ffn_backward_kernel,
        grid_spec=pltpu.PrefetchScalarGridSpec(
            num_scalar_prefetch=1,
            grid=(steps,),
            in_specs=[
                whole,
                whole,
                block,
                block,
                pl.BlockSpec((step, width), lambda i, core_ref: (unit(i, core_ref), 0)),
                pl.BlockSpec((width, step), lambda i, core_ref: (0, unit(i, core_ref))),
            ],
            out_specs=[
                pl.BlockSpec((step, width), lambda i, core_ref: (jnp.minimum(i, half - 1), 0)),
                pl.BlockSpec((step, width), lambda i, core_ref: (jnp.maximum(i - half, 0), 0)),
                up_block,
                up_block,
                pl.BlockSpec((1, step), lambda i, core_ref: (0, unit(i, core_ref))),
                whole,
            ],
            scratch_shapes=[pltpu.VMEM((width, rows), jnp.bfloat16)],
        ),
        out_shape=[
            jax.ShapeDtypeStruct((units // 2, width), jnp.bfloat16),
            jax.ShapeDtypeStruct((units // 2, width), jnp.bfloat16),
            jax.ShapeDtypeStruct((width // 2, units), jnp.bfloat16),
            jax.ShapeDtypeStruct((width // 2, units), jnp.bfloat16),
            jax.ShapeDtypeStruct((1, units), jnp.float32),
            jax.ShapeDtypeStruct((rows, width), jnp.float32),
        ],
        compiler_params=pltpu.CompilerParams(
            dimension_semantics=("arbitrary",), vmem_limit_bytes=VMEM_LIMIT
        ),
        cost_estimate=pl.CostEstimate(flops=1, bytes_accessed=1, transcendentals=0),
        name="ffn_backward",
    )(core, grad_ffn, hidden_two, act, slope, w_down, w_up)


def half_products_kernel(counts, has_came, core_ref, *refs):
    n_in = 2 * sum(counts) + has_came
    given, out_ref = refs[:n_in], refs[n_in]
    held, out_held, in_sems, out_sems = refs[n_in + 1 : 2 * n_in + 1], *refs[2 * n_in + 1 :]
    coming = [
        pltpu.make_async_copy(source, target, in_sems.at[i])
        for i, (source, target) in enumerate(zip(given, held))
    ]
    if has_came:
        coming[-1].start()
    for copy in coming[: n_in - has_came]:
        copy.start()
    going = []
    at = 0
    for term, count in enumerate(counts):
        total = 0.0
        for pair in range(count):
            for copy in coming[at : at + 2]:
                copy.wait()
            left, right = held[at], held[at + 1]
            at += 2
            quarter = left.shape[1] // 4
            spots = [
                pl.ds(pl.multiple_of((2 * x + core_ref[0]) * quarter, quarter), quarter)
                for x in (0, 1)
            ]
            picked = jnp.concatenate([left[:, spot] for spot in spots], 1)
            total = total + product_tn(picked, right[...])
        if has_came:
            if term == 0:
                coming[-1].wait()
            total = total + held[-1][term].astype(jnp.float32)
        out_held[term] = total.astype(jnp.bfloat16)
        copy = pltpu.make_async_copy(out_held.at[term], out_ref.at[term], out_sems.at[term])
        copy.start()
        going.append(copy)
    for copy in going:
        copy.wait()


def half_products(core, terms, came=None):
    arrays = [matrix for pairs in terms for pair in pairs for matrix in pair]
    shape = (len(terms), arrays[0].shape[1] // 2, arrays[1].shape[1])
    given = arrays if came is None else [*arrays, came]
    return pl.pallas_call(
        functools.partial(
            half_products_kernel, tuple(len(pairs) for pairs in terms), came is not None
        ),
        in_specs=[pl.BlockSpec(memory_space=pltpu.SMEM)]
        + [pl.BlockSpec(memory_space=pl.ANY)] * len(given),
        out_specs=pl.BlockSpec(memory_space=pl.ANY),
        out_shape=jax.ShapeDtypeStruct(shape, jnp.bfloat16),
        scratch_shapes=[pltpu.VMEM(array.shape, jnp.bfloat16) for array in given]
        + [
            pltpu.VMEM(shape, jnp.bfloat16),
            pltpu.SemaphoreType.DMA((len(given),)),
            pltpu.SemaphoreType.DMA((len(terms),)),
        ],
        compiler_params=pltpu.CompilerParams(vmem_limit_bytes=VMEM_LIMIT),
        cost_estimate=pl.CostEstimate(flops=1, bytes_accessed=1, transcendentals=0),
        name="half_products",
    )(core, *given)


def column_sum(matrix):
    return jnp.sum(matrix.astype(jnp.float32), 0)


def layer_norm(residual, gain_vec, shift_vec):
    row_mean = jnp.mean(residual, -1, keepdims=True)
    centred = residual - row_mean
    row_var = jnp.mean(centred * centred, -1, keepdims=True)
    return centred * lax.rsqrt(row_var + 1e-05) * gain_vec + shift_vec


def layer_norm_back(residual, gain_vec, grad):
    row_mean = jnp.mean(residual, -1, keepdims=True)
    centred = residual - row_mean
    row_var = jnp.mean(centred * centred, -1, keepdims=True)
    inverse = lax.rsqrt(row_var + 1e-05)
    xhat = centred * inverse
    dx = grad * gain_vec
    inner = dx - jnp.mean(dx, -1, keepdims=True) - xhat * jnp.mean(dx * xhat, -1, keepdims=True)
    return inner * inverse, jnp.sum(grad * xhat, 0), jnp.sum(grad, 0)


SWAP = ((0, 1), (1, 0))


def swap(value, axis):
    return lax.ppermute(value, axis, SWAP)


class RowSum:
    def __init__(self, part):
        self.part, self.names, self.coming = part, ["y", "z", "w"], None

    def pick(self, flip):
        axis = self.names[0]
        return lax.dynamic_index_in_dim(
            self.part, lax.axis_index(axis) ^ flip, "wzy".index(axis), keepdims=False
        )

    def operands(self):
        part = self.pick(1)
        return [part.reshape(-1, part.shape[-1])]

    def launch(self, operands):
        self.coming = swap(operands[0], self.names[0])

    def add(self):
        part = self.pick(0)
        total = part.astype(jnp.float32) + self.coming.reshape(part.shape).astype(jnp.float32)
        self.names.pop(0)
        self.part = total.astype(jnp.bfloat16) if self.names else total
        self.coming = None

    def finish(self):
        while self.names:
            if self.coming is None:
                self.launch(self.operands())
            self.add()
        return self.part


class WeightSum:
    def __init__(self, other, mine):
        self.other, self.mine = other, mine
        self.names, self.coming = ["c", "xy", "yx", "z", "w"], None

    def operands(self):
        if self.names[0] == "c":
            return [self.other]
        parts = [self.pick(side, 1) for side in range(len(self.sides))]
        return [part.reshape(-1, part.shape[-1]) for part in parts]

    def pick(self, side, flip):
        stage = self.names[0]
        dim = {"xy": (1, 4), "yx": (3, 1), "z": (2,), "w": (1,)}[stage][side]
        here = lax.axis_index(stage[side]) ^ flip
        return lax.dynamic_index_in_dim(self.sides[side], here, dim, keepdims=False)

    def launch(self, operands):
        self.coming = [swap(operand, axis) for operand, axis in zip(operands, self.names[0])]

    def add(self):
        f32, bf16 = jnp.float32, jnp.bfloat16
        stage, coming = self.names[0], self.coming
        if stage == "c":
            total = self.mine(coming[0])
            terms, rows, width = total.shape
            total = total.reshape(terms, 2, 2, 2, 2, rows // 16, width)
            self.sides = [total[..., : width // 2], total[..., width // 2 :]]
        else:
            kept = [self.pick(side, 0) for side in range(len(coming))]
            self.sides = [
                part.astype(f32) + came.reshape(part.shape).astype(f32)
                for part, came in zip(kept, coming)
            ]
            if stage != "w":
                self.sides = [side.astype(bf16) for side in self.sides]
            if stage == "yx":
                self.sides = [jnp.concatenate(self.sides, -1)]
        self.names.pop(0)
        self.coming = None

    def finish(self):
        while self.names:
            if self.coming is None:
                self.launch(self.operands())
            self.add()
        return self.sides[0]


class Whole:
    def __init__(self, axes, parts):
        self.names, self.coming = [], None
        self.parts = [
            lax.psum_scatter(part.astype(jnp.bfloat16), axes, scatter_dimension=0, tiled=True)
            for part in parts
        ]

    def finish(self):
        return jnp.stack(self.parts).astype(jnp.float32)


def begin(value, *transfers):
    live = [t for t in transfers if t.names]
    if not live:
        return value
    value, operands = lax.optimization_barrier((value, [t.operands() for t in live]))
    for t, ready in zip(live, operands):
        t.launch(ready)
    return value


def advance(value, *transfers):
    live = [t for t in transfers if t.coming is not None]
    if not live:
        return value
    value, arrived = lax.optimization_barrier((value, [t.coming for t in live]))
    for t, coming in zip(live, arrived):
        t.coming = coming
        t.add()
    return begin(value, *live)


class Rows:
    def __init__(self, part):
        self.part, self.names, self.coming = part, (), None

    def finish(self):
        return self.part.astype(jnp.float32)


class Known:
    def __init__(self, parts):
        self.parts, self.names, self.coming = parts, (), None

    def finish(self, place):
        return self.parts


class RowGathering:
    def __init__(self, block, cuts):
        self.block, self.cuts, self.names = block, cuts, ["w", "z", "y"]
        self.coming = None

    def operands(self):
        return [self.block]

    def launch(self, operands):
        (self.block,) = operands
        self.coming = swap(self.block, self.names[0])

    def add(self):
        self.names.pop(0)
        self.block = jnp.stack([self.block, self.coming])
        self.coming = None

    def finish(self, place):
        while self.names:
            if self.coming is None:
                self.launch(self.operands())
            self.add()
        return assemble_rows(place, self.cuts, self.block)


def put_blocks(own, source, spans, outs, lead):
    shard = source.shape[-2]
    for y, z, w in itertools.product(range(2), range(2), range(2)):
        place = ((own[0] ^ w) * 2 + (own[1] ^ z)) * 2 + (own[2] ^ y)
        rows = pl.ds(pl.multiple_of(place * shard, shard), shard)
        for first, out, column, count in spans:
            outs[out][rows, column : column + count] = source[
                (*lead(y), z, w, slice(None), slice(first, first + count))
            ]


def assemble_kernel(spans, place_ref, left_own, right_own, left_came, right_came, *outs):
    own = (place_ref[2], place_ref[3], place_ref[4])
    core = pl.program_id(0)
    for which, left, right in ((0, left_own, right_own), (1, left_came, right_came)):

        @pl.when(core == which)
        def _(left=left, right=right):
            put_blocks(own, left, spans[0], outs, lambda y: (0, y))
            put_blocks(own, right, spans[1], outs, lambda y: (y, 0))


def assemble(place, spans, arrays, shapes):
    left_own, right_own, _, _ = arrays
    shard = left_own.shape[-2]

    def left_spec(which):
        def at(core, x, _):
            return (jnp.where(core == which, x, 1 - which), 0, 0, 0, 0, 0)

        return pl.BlockSpec((1, 2, 2, 2, shard, left_own.shape[-1]), at)

    def right_spec(which):
        def at(core, x, _):
            return (0, jnp.where(core == which, x, 1 - which), 0, 0, 0, 0)

        return pl.BlockSpec((2, 1, 2, 2, shard, right_own.shape[-1]), at)

    def out_at(core, x, place_ref):
        return ((place_ref[0] ^ x) * 2 + (place_ref[1] ^ core), 0)

    return pl.pallas_call(
        functools.partial(assemble_kernel, spans),
        grid_spec=pltpu.PrefetchScalarGridSpec(
            num_scalar_prefetch=1,
            grid=(2, 2),
            in_specs=[left_spec(0), right_spec(0), left_spec(1), right_spec(1)],
            out_specs=[pl.BlockSpec((8 * shard, shape[1]), out_at) for shape in shapes],
        ),
        out_shape=[jax.ShapeDtypeStruct(shape, jnp.bfloat16) for shape in shapes],
        compiler_params=pltpu.CompilerParams(
            dimension_semantics=("arbitrary", "arbitrary"), vmem_limit_bytes=VMEM_LIMIT
        ),
        cost_estimate=pl.CostEstimate(
            flops=0, transcendentals=0, bytes_accessed=sum(4 * array.size for array in arrays)
        ),
        name="assemble",
    )(place, *arrays)


def assemble_rows_kernel(cuts, place_ref, source, *outs):
    own = (place_ref[2], place_ref[3], place_ref[4])
    for out, (first, count) in zip(outs, cuts):
        for y, z, w in itertools.product(range(2), range(2), range(2)):
            block = ((own[0] ^ w) * 2 + (own[1] ^ z)) * 2 + (own[2] ^ y)
            rows = pl.ds(pl.multiple_of(block * count, count), count)
            out[rows, :] = source[y, z, w, first : first + count, :]


def assemble_rows(place, cuts, gathered):
    width = gathered.shape[-1]
    return pl.pallas_call(
        functools.partial(assemble_rows_kernel, cuts),
        in_specs=[pl.BlockSpec(memory_space=pltpu.SMEM), pl.BlockSpec(memory_space=pltpu.VMEM)],
        out_specs=[pl.BlockSpec(memory_space=pltpu.VMEM) for _ in cuts],
        out_shape=[jax.ShapeDtypeStruct((8 * count, width), jnp.bfloat16) for _, count in cuts],
        compiler_params=pltpu.CompilerParams(vmem_limit_bytes=VMEM_LIMIT),
        cost_estimate=pl.CostEstimate(
            flops=0, transcendentals=0, bytes_accessed=4 * gathered.size
        ),
        name="assemble_rows",
    )(place, gathered)


class Gathering:
    def __init__(self, block, cut, spans, shapes):
        self.sides, self.cut = [block], cut
        self.spans, self.shapes = spans, shapes
        self.names, self.coming = ["w", "z", "yx", "xy", "cc"], None

    def operands(self):
        return self.sides

    def launch(self, operands):
        self.sides = operands
        self.coming = [swap(side, axis) for side, axis in zip(operands, self.names[0])]

    def add(self):
        stage = self.names.pop(0)
        coming, self.coming = self.coming, None
        if stage == "cc":
            self.arrived = coming
        elif stage == "z":
            pair = [self.sides[0], coming[0]]
            self.sides = [
                jnp.stack([block[..., : self.cut] for block in pair]),
                jnp.stack([block[..., self.cut :] for block in pair]),
            ]
        else:
            self.sides = [jnp.stack(pair) for pair in zip(self.sides, coming)]

    def finish(self, place):
        while self.names:
            if self.coming is None:
                self.launch(self.operands())
            self.add()
        return assemble(place, self.spans, [*self.sides, *self.arrived], self.shapes)


class Links:
    def __init__(self, mesh):
        self.fast = dict(mesh.shape) == {"fsdp": 4, "ctx": 8}
        if self.fast:
            self.mesh = Mesh(mesh.devices.reshape(2, 2, 2, 2, 2), ("x", "c", "w", "z", "y"))
            self.rows, self.ctx = ("x", "c"), ("w", "z", "y")
        else:
            self.mesh, self.rows, self.ctx = mesh, ("fsdp",), ("ctx",)
        self.every = self.rows + self.ctx

    def place(self):
        axes = self.every if self.fast else ()
        return jnp.stack([lax.axis_index(axis).astype(jnp.int32) for axis in axes or self.rows])

    def gather(self, weights, cut):
        if not self.fast:
            return Known([lax.all_gather(w, self.every, axis=0, tiled=True) for w in weights])
        shapes = tuple((32 * w.shape[0], w.shape[1]) for w in weights)
        block = weights[0] if len(weights) == 1 else jnp.concatenate(weights, 1)
        first, left, right = 0, [], []
        for out, weight in enumerate(weights):
            count = weight.shape[1]
            low = min(max(cut - first, 0), count)
            if low:
                left.append((first, out, 0, low))
            if low < count:
                right.append((first + low - cut, out, low, count - low))
            first += count
        return Gathering(block, cut, (tuple(left), tuple(right)), shapes)

    def gather_once(self, weights):
        return lax.all_gather(jnp.concatenate(weights, 1), self.every, axis=0, tiled=True)

    def gather_rows(self, parts):
        if not self.fast:
            return Known([lax.all_gather(part, self.ctx, axis=0, tiled=True) for part in parts])
        cuts, first = [], 0
        for part in parts:
            cuts.append((first, part.shape[0]))
            first += part.shape[0]
        return RowGathering(jnp.concatenate(parts, 0), tuple(cuts))

    def weight_sum(self, terms):
        if not self.fast:
            return Whole(
                self.every,
                [sum(product_tn(left, right) for left, right in pairs) for pairs in terms],
            )
        core = lax.axis_index("c").astype(jnp.int32).reshape(1)
        return WeightSum(
            half_products(1 - core, terms), lambda came: half_products(core, terms, came)
        )

    def row_sum(self, part):
        part = part.astype(jnp.bfloat16)
        if not self.fast:
            return Rows(lax.psum_scatter(part, self.ctx, scatter_dimension=0, tiled=True))
        return RowSum(part.reshape(2, 2, 2, part.shape[0] // 8, part.shape[1]))


def body(
    links,
    prompt_in,
    cont_in,
    encoder,
    prompt_start,
    cont_start,
    self_proj,
    self_out,
    cross_query,
    cross_kv,
    cross_out,
    up_proj,
    down_proj,
    vec_bias,
    up_bias,
    ln_gain,
    ln_bias,
    prompt_cot,
    cont_cot,
):
    f32, bf16 = jnp.float32, jnp.bfloat16
    shard, width = self_out.shape
    prompt_rows, slot_len = prompt_in.shape[1], cont_in.shape[2]
    block_index = lax.axis_index(links.ctx)
    ctx_count = lax.axis_size(links.ctx)
    prompt_len = prompt_rows * ctx_count
    enc_rows = encoder.shape[1]
    hidden = up_bias.shape[0] // shard
    scale = HDIM ** (-0.5)

    small = jnp.concatenate(
        [vec_bias.T, ln_gain.T, ln_bias.T, up_bias.reshape(hidden, shard).T], 1
    )
    small = jnp.pad(small, ((0, 0), (0, 128 - small.shape[1])))
    place = links.place()
    rows_in = links.gather_rows([prompt_in[0], encoder[0]])
    first = links.gather([self_proj, small], 13 * 128)
    second = links.gather([self_out, cross_query, cross_kv, cross_out], 20 * 128)
    up = links.gather([up_proj], 16 * 128)
    tokens = jnp.concatenate([prompt_in[0], cont_in[0, 0]], 0)
    tokens = begin(tokens, first, rows_in)
    tokens = advance(tokens, first)
    tokens = advance(tokens, rows_in)
    tokens = advance(tokens, first)
    tokens = begin(tokens, second)
    tokens = advance(tokens, first)
    tokens = advance(tokens, rows_in, second)
    tokens = advance(tokens, first)
    tokens = begin(tokens, up)
    tokens = advance(tokens, first)
    self_w, small = first.finish(place)
    w_q, w_kv = self_w[:, :width], self_w[:, width:]
    small = small.astype(f32).T
    biases, gains, shifts = small[:7], small[7:10], small[10:13]
    hidden_bias = (
        small[13 : 13 + hidden]
        .reshape(hidden, width // shard, shard)
        .transpose(1, 0, 2)
        .reshape(hidden * width)
    )

    every_begin = cont_start[0]
    own_begin = lax.dynamic_index_in_dim(every_begin, block_index, 0, keepdims=False)
    scalars = jnp.stack([prompt_start[0], own_begin, block_index.astype(jnp.int32)])
    cont_rows = tokens[prompt_rows:]
    row_total = tokens.shape[0]
    row_spot = jnp.arange(row_total, dtype=jnp.int32)
    valid_rows = jnp.where(
        row_spot < prompt_rows,
        block_index * prompt_rows + row_spot >= prompt_start[0],
        row_spot - prompt_rows >= own_begin,
    ).astype(f32)[:, None]
    valid_count = (prompt_len - prompt_start[0] + jnp.sum(slot_len - every_begin)).astype(f32)

    kv_bias = jnp.concatenate([jnp.zeros((width,), f32), biases[1]])
    queries = ((product(tokens, w_q) + biases[0]) * scale).astype(bf16)
    cont_kv = (product(cont_rows, w_kv) + kv_bias).astype(bf16)
    (queries, cont_kv) = advance((queries, cont_kv), second, up)
    queries = advance(queries, rows_in)
    prompt_all, enc_all = rows_in.finish(place)
    prompt_kv = (product(prompt_all, w_kv) + kv_bias).astype(bf16)
    plan = self_plan(prompt_rows, prompt_len, slot_len)
    prompt_kv, down_proj = advance((prompt_kv, down_proj), second, up)
    w_down = lax.all_gather(down_proj, links.every, axis=0, tiled=True)
    attn, self_log = attend_forward(scalars, queries, [prompt_kv, cont_kv], plan, prompt_rows)
    attn = advance(attn, second)
    attn = advance(attn, second, up)
    w_so, w_cq, w_ckv, w_co = second.finish(place)
    branch_self = product(attn, w_so) + biases[2]
    resid_one = tokens.astype(f32) + branch_self
    hidden_one = layer_norm(resid_one, gains[0], shifts[0]).astype(bf16)

    enc_bias = jnp.concatenate([jnp.zeros((width,), f32), biases[4]])
    enc_kv = (product(enc_all, w_ckv) + enc_bias).astype(bf16)
    cross_queries = ((product(hidden_one, w_cq) + biases[3]) * scale).astype(bf16)
    enc_len = enc_all.shape[0]
    cross_attn, cross_log = attend_forward(
        None, cross_queries, [enc_kv], cross_plan(row_total, enc_len, 320), 0
    )
    cross_attn = advance(cross_attn, up)
    branch_cross = product(cross_attn, w_co) + biases[5]
    resid_two = hidden_one.astype(f32) + branch_cross
    hidden_two = layer_norm(resid_two, gains[1], shifts[1]).astype(bf16)
    hidden_two = advance(hidden_two, up)
    (w_up,) = up.finish(place)

    act, slope, branch_ffn = ffn_forward(hidden_two, w_up, hidden_bias, w_down)
    branch_ffn = branch_ffn + biases[6]
    resid_three = hidden_two.astype(f32) + branch_ffn
    output = layer_norm(resid_three, gains[2], shifts[2]).astype(bf16)

    members = (tokens, branch_self, hidden_one, branch_cross, hidden_two, branch_ffn)
    squares = jnp.stack(
        [jnp.sum(valid_rows * jnp.square(member.astype(f32)), 0) for member in members]
    )
    grad_out = jnp.concatenate([prompt_cot[0], cont_cot[0, 0]], 0).astype(f32)
    grad_three, gain_three, shift_three = layer_norm_back(resid_three, gains[2], grad_out)
    grad_ffn = grad_three.astype(bf16)
    half_width = width // 2
    if links.fast:
        core = lax.axis_index("c").astype(jnp.int32).reshape(1)
        down_other, down_mine, up_other, up_mine, up_bias_part, back_ffn = ffn_backward(
            core, grad_ffn, hidden_two, act, slope, w_down, w_up
        )

        def add_to(mine):
            return lambda came: (mine.astype(f32) + came[0].astype(f32)).astype(bf16)[None]

        down_sum = WeightSum(down_other[None], add_to(down_mine))
        up_sum = WeightSum(up_other[None], add_to(up_mine))
    else:
        grad_pre = (product_nt(grad_ffn, w_down) * slope.astype(f32)).astype(bf16)
        down_sum = links.weight_sum([[(act, grad_ffn)]])
        up_sum = links.weight_sum([[(hidden_two, grad_pre)]])
        up_bias_part = column_sum(grad_pre)
        back_ffn = product_nt(grad_pre, w_up)
    back_ffn = begin(back_ffn, down_sum, up_sum)
    grad_hidden_two = grad_three + back_ffn
    grad_two, gain_two, shift_two = layer_norm_back(resid_two, gains[1], grad_hidden_two)
    grad_cross = grad_two.astype(bf16)
    grad_cattn = product_nt(grad_cross, w_co).astype(bf16)
    grad_cattn = advance(grad_cattn, down_sum)
    cross_gq, cross_gk, cross_gv = attend_backward(
        None,
        cross_queries,
        grad_cattn,
        cross_attn,
        cross_log,
        [enc_kv],
        cross_plan(row_total, enc_len, 384),
        0,
        512,
        (0,),
    )
    cross_gq = advance(cross_gq, down_sum, up_sum)
    grad_cq = (cross_gq.astype(f32) * scale).astype(bf16)
    enc_back = product_nt(cross_gk[0], w_ckv[:, :width]) + product_nt(
        cross_gv[0], w_ckv[:, width:]
    )
    enc_sum = links.row_sum(enc_back)
    grad_hidden_one = grad_two + product_nt(grad_cq, w_cq)
    grad_one, gain_one, shift_one = layer_norm_back(resid_one, gains[0], grad_hidden_one)
    grad_self = grad_one.astype(bf16)
    mid_sum = links.weight_sum(
        [
            [(cross_attn, grad_cross)],
            [(hidden_one, grad_cq)],
            [(attn, grad_self)],
            [(enc_all, cross_gk[0])],
            [(enc_all, cross_gv[0])],
        ]
    )
    if links.fast:
        grad_self, mid_sum.other = advance((grad_self, mid_sum.other), down_sum, up_sum)
    grad_self = begin(grad_self, mid_sum)
    grad_attn = product_nt(grad_self, w_so).astype(bf16)
    small_part = jnp.concatenate(
        [
            squares,
            jnp.stack(
                [
                    column_sum(grad_self),
                    column_sum(grad_cq),
                    column_sum(cross_gv[0]),
                    column_sum(grad_cross),
                    column_sum(grad_ffn),
                    gain_one,
                    gain_two,
                    gain_three,
                    shift_one,
                    shift_two,
                    shift_three,
                ]
            ),
            up_bias_part.reshape(width // shard, hidden, shard)
            .transpose(1, 0, 2)
            .reshape(hidden, width),
        ],
        0,
    )
    grad_attn, small_part = lax.optimization_barrier((grad_attn, small_part))
    grad_attn = advance(grad_attn, mid_sum)
    self_args = (queries, grad_attn, attn, self_log, [prompt_kv, cont_kv], plan, prompt_rows)
    part_gq, prompt_gk, prompt_gv = attend_backward(scalars, *self_args, 1024, (0,))
    prompt_gk, prompt_gv = prompt_gk[0], prompt_gv[0]
    w_k, w_v = w_kv[:, :width], w_kv[:, width:]
    part_gq = advance(part_gq, up_sum, mid_sum, down_sum)
    prompt_sum = links.row_sum(product_nt(prompt_gk, w_k) + product_nt(prompt_gv, w_v))
    part_gq = begin(part_gq, prompt_sum)
    self_gq, cont_gk, cont_gv = attend_backward(scalars, *self_args, 512, (1,), part_gq)
    cont_gk, cont_gv = cont_gk[0], cont_gv[0]
    self_gq = advance(self_gq, down_sum, up_sum, mid_sum, prompt_sum)
    self_gq = begin(self_gq, enc_sum)
    grad_q = (self_gq.astype(f32) * scale).astype(bf16)

    last_part = jnp.stack([column_sum(grad_q), column_sum(prompt_gv) + column_sum(cont_gv)])
    small_part = jnp.concatenate(
        [small_part, last_part, jnp.zeros((32 - small_part.shape[0] - 2, width), f32)], 0
    )
    small_all = lax.all_gather(small_part, links.every, axis=0, tiled=True)
    self_sum = links.weight_sum(
        [
            [(tokens, grad_q)],
            [(prompt_all, prompt_gk), (cont_rows, cont_gk)],
            [(prompt_all, prompt_gv), (cont_rows, cont_gv)],
        ]
    )
    input_grad = grad_one + product_nt(grad_q, w_q)
    cont_grad = input_grad[prompt_rows:] + product_nt(cont_gk, w_k) + product_nt(cont_gv, w_v)
    if links.fast:
        cont_grad, self_sum.other = advance(
            (cont_grad, self_sum.other), mid_sum, prompt_sum, up_sum
        )
    cont_grad = begin(cont_grad, self_sum)
    cont_grad = advance(cont_grad, self_sum, enc_sum)
    cont_grad = advance(cont_grad, self_sum, mid_sum, prompt_sum)
    cont_grad = advance(cont_grad, self_sum, enc_sum)
    cont_grad = advance(cont_grad, self_sum, enc_sum)
    cont_grad = cont_grad[None, None]
    prompt_grad = (input_grad[:prompt_rows] + prompt_sum.finish())[None]
    encoder_grad = enc_sum.finish()[None]
    up_total, down_total = up_sum.finish()[0], down_sum.finish()[0]
    co_total, cq_total, so_total, ck_total, cv_total = mid_sum.finish()
    ckv_total = jnp.concatenate([ck_total, cv_total], 1)
    sin_total = jnp.concatenate([*self_sum.finish()], 1)
    small_all = small_all.reshape(-1, ctx_count, 32, width)
    group = lax.axis_index(links.rows)
    squares = jnp.sum(lax.dynamic_index_in_dim(small_all, group, 0, keepdims=False)[:, :6], (0, 2))
    statistics = (squares / (valid_count * width))[None]
    at = lax.axis_index(links.every) * shard
    sums = jnp.sum(lax.dynamic_slice_in_dim(small_all, at, shard, 3), (0, 1))
    bias_total = jnp.concatenate([sums[21:23], sums[6:11]])
    gain_total, shift_total = sums[11:14], sums[14:17]
    up_bias_total = sums[17 : 17 + hidden].reshape(hidden * shard)
    return (
        output[:prompt_rows][None],
        output[prompt_rows:][None, None],
        prompt_grad,
        cont_grad,
        encoder_grad,
        sin_total,
        so_total,
        cq_total,
        ckv_total,
        co_total,
        up_total,
        down_total,
        bias_total,
        up_bias_total,
        gain_total,
        shift_total,
        statistics,
    )


def solution(mesh):
    links = Links(mesh)
    fs, ctx, every = links.rows, links.ctx, links.every
    group = P(fs, ctx, None)
    slots = P(fs, ctx, None, None)
    weight = P(every, None)
    vectors = P(None, every)
    return jax.shard_map(
        functools.partial(body, links),
        mesh=links.mesh,
        in_specs=(group, slots, group, P(fs), P(fs, None))
        + (weight,) * 7
        + (vectors, P(every), vectors, vectors, group, slots),
        out_specs=(group, slots, group, slots, group)
        + (weight,) * 7
        + (vectors, P(every), vectors, vectors, P(fs, None)),
        check_vma=False,
    )
```

```python
import functools
import itertools

import jax
import jax.numpy as jnp
from jax import lax
from jax.experimental import pallas as pl
from jax.experimental.pallas import tpu as pltpu
from jax.sharding import Mesh
from jax.sharding import PartitionSpec as P

HEADS = 16
HDIM = 64
MASKED = -1e30


def product(first_mat, second_mat):
    return jnp.dot(first_mat, second_mat, preferred_element_type=jnp.float32)


def product_tn(first_mat, second_mat):
    return lax.dot_general(
        first_mat, second_mat, (((0,), (0,)), ((), ())), preferred_element_type=jnp.float32
    )


def product_nt(first_mat, second_mat):
    return lax.dot_general(
        first_mat, second_mat, (((1,), (1,)), ((), ())), preferred_element_type=jnp.float32
    )


def bias_fill(sc_ref, prompt_bias, own_bias, flip, segs=(0, 1)):
    begin, cont_begin, block = sc_ref[0], sc_ref[1], sc_ref[2]
    q_dim, k_dim = (1, 0) if flip else (0, 1)
    if 0 in segs:
        shape = prompt_bias.shape
        rows = shape[q_dim]
        spot = lax.broadcasted_iota(jnp.int32, shape, q_dim) + block * rows
        key = lax.broadcasted_iota(jnp.int32, shape, k_dim)
        seen = (key <= spot) & ((key >= begin) | (key == spot))
        prompt_bias[...] = jnp.where(seen, 0.0, MASKED)
    if 1 in segs:
        shape = own_bias.shape
        spot = lax.broadcasted_iota(jnp.int32, shape, q_dim)
        key = lax.broadcasted_iota(jnp.int32, shape, k_dim)
        seen = (key <= spot) & ((key >= cont_begin) | (key == spot))
        own_bias[...] = jnp.where(seen, 0.0, MASKED)


def self_plan(prompt_rows, prompt_len, slot_len):
    step = slot_len // 2
    return (
        (0, prompt_rows, ((0, prompt_len, "prompt"),)),
        (prompt_rows, step, ((0, prompt_len, "start"), (1, step, "own"))),
        (prompt_rows + step, slot_len - step, ((0, prompt_len, "start"), (1, slot_len, "own"))),
    )


def cross_plan(row_total, key_total, step):
    return tuple(
        (at, min(step, row_total - at), ((0, key_total, None),)) for at in range(0, row_total, step)
    )


def head_lanes(head):
    lane = lax.broadcasted_iota(jnp.int32, (1, 2 * HDIM), 1)
    return (lane >= head * HDIM) & (lane < (head + 1) * HDIM)


def only(block, lanes):
    return jnp.where(lanes, block, jnp.zeros_like(block))


def fwd_kernel(plan, masked, slot_at, *refs):
    n_seg = 2 if masked else 1
    if masked:
        sc_ref, refs = refs[0], refs[1:]
    q_ref = refs[0]
    k_refs, v_refs = refs[1 : 1 + n_seg], refs[1 + n_seg : 1 + 2 * n_seg]
    o_ref, lse_ref = refs[1 + 2 * n_seg : 3 + 2 * n_seg]
    pair = pl.program_id(0)
    if masked:
        prompt_bias, own_bias = refs[3 + 2 * n_seg :]

        @pl.when(pair == 0)
        def _():
            bias_fill(sc_ref, prompt_bias, own_bias, False)

    out_lane = lax.broadcasted_iota(jnp.int32, (1, 128), 1)
    for q_at, q_n, parts in plan:
        rows = slice(q_at, q_at + q_n)
        q_blk = q_ref[rows, :]
        mixed_pair = None
        for head in (0, 1):
            lanes = head_lanes(head)
            q_one = only(q_blk, lanes)
            scores = []
            for seg, k_n, kind in parts:
                part = product_nt(q_one, k_refs[seg][:k_n, :])
                if kind == "prompt":
                    part = part + prompt_bias[...]
                elif kind == "own":
                    at = q_at - slot_at
                    part = part + own_bias[at : at + q_n, :k_n]
                elif kind == "start":
                    key = lax.broadcasted_iota(jnp.int32, (1, 128), 1)
                    first = jnp.where(key >= sc_ref[0], part[:, :128], MASKED)
                    part = jnp.concatenate([first, part[:, 128:]], 1)
                scores.append(part)
            row_max = functools.reduce(
                jnp.maximum, [jnp.max(part, 1, keepdims=True) for part in scores]
            )
            totals, mixed = 0.0, 0.0
            for part, (seg, k_n, _) in zip(scores, parts):
                shifted = jnp.exp(part - row_max)
                totals = totals + jnp.sum(shifted, 1, keepdims=True)
                mixed = mixed + product(shifted.astype(jnp.bfloat16), v_refs[seg][:k_n, :])
            mixed = mixed / totals
            mixed_pair = mixed if head == 0 else jnp.where(lanes, mixed, mixed_pair)
            lse = row_max + jnp.log(totals)
            lse_ref[rows, :] = jnp.where(out_lane == 2 * pair + head, lse, lse_ref[rows, :])
        o_ref[rows, :] = mixed_pair.astype(jnp.bfloat16)


def accumulate(total_ref, keys, done, part):
    known = min(max(done - keys.start, 0), keys.stop - keys.start)
    if known:
        total_ref[keys.start : keys.start + known, :] += part[:known]
    if known < keys.stop - keys.start:
        total_ref[keys.start + known : keys.stop, :] = part[known:]


def bwd_kernel(plan, masked, slot_at, key_step, segs, onto, *refs):
    n_seg = len(segs)
    if masked:
        sc_ref, refs = refs[0], refs[1:]
    q_ref, g_ref, o_ref, lse_ref = refs[:4]
    k_refs, v_refs = refs[4 : 4 + n_seg], refs[4 + n_seg : 4 + 2 * n_seg]
    outs = refs[4 + 2 * n_seg :]
    if onto:
        dq_in, outs = outs[0], outs[1:]
        dq_in_rows = slice(0, plan[0][0])
        outs[0][dq_in_rows, :] = dq_in[dq_in_rows, :].astype(outs[0].dtype)
    dq_ref, dk_refs, dv_refs = outs[0], outs[1 : 1 + n_seg], outs[1 + n_seg : 1 + 2 * n_seg]
    scratch = outs[1 + 2 * n_seg :]
    dk_acc, dv_acc = scratch[:n_seg], scratch[n_seg : 2 * n_seg]
    pair = pl.program_id(0)
    if masked:
        prompt_bias, own_bias = scratch[2 * n_seg :]

        @pl.when(pair == 0)
        def _():
            bias_fill(sc_ref, prompt_bias, own_bias, True, segs)

    done = [0] * n_seg
    picks = jnp.concatenate(
        [only(jnp.ones((1, 2 * HDIM), jnp.float32), head_lanes(h)) for h in (0, 1)]
        + [jnp.zeros((6, 2 * HDIM), jnp.float32)],
        0,
    )
    for q_at, q_n, parts in plan:
        rows = slice(q_at, q_at + q_n)
        q_blk, g_blk = q_ref[rows, :], g_ref[rows, :]
        inner = lax.dot_general(
            picks,
            g_blk.astype(jnp.float32) * o_ref[rows, :].astype(jnp.float32),
            (((1,), (1,)), ((), ())),
            precision=lax.Precision.HIGHEST,
            preferred_element_type=jnp.float32,
        )
        dq = dq_in[rows, :] if onto else 0.0
        for head in (0, 1):
            lanes = head_lanes(head)
            q_one, g_one = only(q_blk, lanes), only(g_blk, lanes)
            lse = lse_ref[0, head : head + 1, rows]
            row_inner = inner[head : head + 1, :]
            for which, k_n, kind in parts:
                seg = segs.index(which)
                for at in range(0, k_n, key_step):
                    keys = slice(at, min(at + key_step, k_n))
                    k_one = only(k_refs[seg][keys, :], lanes)
                    scores = product_nt(k_one, q_blk)
                    if kind == "prompt":
                        scores = scores + prompt_bias[keys, :]
                    elif kind == "own":
                        q_off = q_at - slot_at
                        scores = scores + own_bias[keys, q_off : q_off + q_n]
                    elif kind == "start" and at == 0:
                        key = lax.broadcasted_iota(jnp.int32, (128, 1), 0)
                        first = jnp.where(key >= sc_ref[0], scores[:128, :], MASKED)
                        scores = jnp.concatenate([first, scores[128:, :]], 0)
                    probs = jnp.exp(scores - lse)
                    grad_probs = product_nt(v_refs[seg][keys, :], g_one)
                    grad_scores = (probs * (grad_probs - row_inner)).astype(jnp.bfloat16)
                    add_v = product(probs.astype(jnp.bfloat16), g_one)
                    add_k = product(grad_scores, q_one)
                    accumulate(dv_acc[seg], keys, done[seg], add_v)
                    accumulate(dk_acc[seg], keys, done[seg], add_k)
                    dq = dq + product_tn(grad_scores, k_one)
                done[seg] = max(done[seg], k_n)
        dq_ref[rows, :] = dq.astype(dq_ref.dtype)
    for seg in range(n_seg):
        dk_refs[seg][...] = dk_acc[seg][...].astype(jnp.bfloat16)
        dv_refs[seg][...] = dv_acc[seg][...].astype(jnp.bfloat16)


VMEM_LIMIT = 48 * 1024 * 1024


def pair_spec(rows, shift=0):
    return pl.BlockSpec((rows, 2 * HDIM), lambda i: (0, i + shift))


def attend_forward(scalars, queries, kv_list, plan, slot_at):
    masked = scalars is not None
    row_total, width = queries.shape
    pairs = width // (2 * HDIM)
    scratch = []
    if masked:
        prompt_len, slot_len = kv_list[0].shape[0], kv_list[1].shape[0]
        scratch = [
            pltpu.VMEM((slot_at, prompt_len), jnp.float32),
            pltpu.VMEM((slot_len, slot_len), jnp.float32),
        ]
    area = sum(q_n * k_n for _, q_n, parts in plan for _, k_n, _ in parts)
    return pl.pallas_call(
        functools.partial(fwd_kernel, plan, masked, slot_at),
        grid=(pairs,),
        in_specs=([pl.BlockSpec(memory_space=pltpu.SMEM)] if masked else [])
        + [pair_spec(row_total)]
        + [pair_spec(kv.shape[0]) for kv in kv_list]
        + [pair_spec(kv.shape[0], pairs) for kv in kv_list],
        out_specs=[pair_spec(row_total), pl.BlockSpec((row_total, 128), lambda i: (0, 0))],
        out_shape=[
            jax.ShapeDtypeStruct((row_total, width), jnp.bfloat16),
            jax.ShapeDtypeStruct((row_total, 128), jnp.float32),
        ],
        scratch_shapes=scratch,
        compiler_params=pltpu.CompilerParams(
            dimension_semantics=("arbitrary",), vmem_limit_bytes=VMEM_LIMIT
        ),
        cost_estimate=pl.CostEstimate(flops=1, bytes_accessed=1, transcendentals=0),
        name="attend_forward",
    )(*([scalars] if masked else []), queries, *kv_list, *kv_list)


def attend_backward(
    scalars, queries, grads, mixed, log_totals, kv_list, plan, slot_at, key_step, segs, onto=None
):
    masked = scalars is not None
    row_total, width = queries.shape
    pairs = width // (2 * HDIM)
    lse = log_totals[:, :HEADS].T.reshape(pairs, 2, row_total)
    plan = tuple(
        (q_at, q_n, kept)
        for q_at, q_n, parts in plan
        if (kept := tuple(part for part in parts if part[0] in segs))
    )
    prompt_len, slot_len = kv_list[0].shape[0], kv_list[-1].shape[0]
    kv_list = [kv_list[seg] for seg in segs]
    scratch = [pltpu.VMEM((kv.shape[0], 2 * HDIM), jnp.float32) for kv in kv_list] * 2
    if masked:
        scratch += [
            pltpu.VMEM((prompt_len if 0 in segs else 8, slot_at), jnp.float32),
            pltpu.VMEM((slot_len, slot_len) if 1 in segs else (8, 128), jnp.float32),
        ]
    area = sum(q_n * k_n for _, q_n, parts in plan for _, k_n, _ in parts)
    n_seg = len(kv_list)
    partial = masked and 1 not in segs
    given = [] if onto is None else [onto]
    outs = pl.pallas_call(
        functools.partial(bwd_kernel, plan, masked, slot_at, key_step, segs, bool(given)),
        grid=(pairs,),
        in_specs=([pl.BlockSpec(memory_space=pltpu.SMEM)] if masked else [])
        + [pair_spec(row_total)] * 3
        + [pl.BlockSpec((1, 2, row_total), lambda i: (i, 0, 0))]
        + [pair_spec(kv.shape[0]) for kv in kv_list]
        + [pair_spec(kv.shape[0], pairs) for kv in kv_list]
        + [pair_spec(row_total)] * len(given),
        out_specs=[pair_spec(row_total)] + [pair_spec(kv.shape[0]) for kv in kv_list] * 2,
        out_shape=[
            jax.ShapeDtypeStruct((row_total, width), jnp.float32 if partial else jnp.bfloat16)
        ]
        + [jax.ShapeDtypeStruct((kv.shape[0], width), jnp.bfloat16) for kv in kv_list] * 2,
        scratch_shapes=scratch,
        compiler_params=pltpu.CompilerParams(
            dimension_semantics=("arbitrary",), vmem_limit_bytes=VMEM_LIMIT
        ),
        cost_estimate=pl.CostEstimate(flops=1, bytes_accessed=1, transcendentals=0),
        name="attend_backward",
    )(*([scalars] if masked else []), queries, grads, mixed, lse, *kv_list, *kv_list, *given)
    return outs[0], outs[1 : 1 + n_seg], outs[1 + n_seg :]
def ffn_forward_kernel(h_ref, up_ref, bias_ref, down_ref, act_ref, slope_ref, out_ref):
    step = pl.program_id(0)
    rows = h_ref.shape[0]
    half = rows // 2
    for at in (0, half):
        part = slice(at, at + half)
        pre = product(h_ref[part, :], up_ref[...]) + bias_ref[...]
        cdf = 0.5 * (1.0 + lax.erf(pre * (0.5**0.5)))
        act = (pre * cdf).astype(jnp.bfloat16)
        act_ref[part, :] = act
        slope = cdf + pre * jnp.exp(-0.5 * pre * pre) * 0.3989422804014327
        slope_ref[part, :] = slope.astype(jnp.bfloat16)
        add = product(act, down_ref[...])

        @pl.when(step == 0)
        def _(part=part, add=add):
            out_ref[part, :] = add

        @pl.when(step > 0)
        def _(part=part, add=add):
            out_ref[part, :] += add


def ffn_forward(hidden_two, w_up, up_bias, w_down, step=1024):
    rows, width = hidden_two.shape
    units = w_up.shape[1]
    whole = pl.BlockSpec((rows, width), lambda i: (0, 0))
    block = pl.BlockSpec((rows, step), lambda i: (0, i))
    return pl.pallas_call(
        ffn_forward_kernel,
        grid=(units // step,),
        in_specs=[
            whole,
            pl.BlockSpec((width, step), lambda i: (0, i)),
            pl.BlockSpec((1, step), lambda i: (0, i)),
            pl.BlockSpec((step, width), lambda i: (i, 0)),
        ],
        out_specs=[block, block, whole],
        out_shape=[
            jax.ShapeDtypeStruct((rows, units), jnp.bfloat16),
            jax.ShapeDtypeStruct((rows, units), jnp.bfloat16),
            jax.ShapeDtypeStruct((rows, width), jnp.float32),
        ],
        compiler_params=pltpu.CompilerParams(
            dimension_semantics=("arbitrary",), vmem_limit_bytes=VMEM_LIMIT
        ),
        cost_estimate=pl.CostEstimate(flops=1, bytes_accessed=1, transcendentals=0),
        name="ffn_forward",
    )(hidden_two, w_up, up_bias.reshape(1, units), w_down)


def ffn_backward_kernel(
    core_ref,
    g_ref,
    h_ref,
    act_ref,
    slope_ref,
    down_ref,
    up_ref,
    down_other,
    down_mine,
    up_other,
    up_mine,
    bias_ref,
    out_ref,
    turned,
):
    step, steps = pl.program_id(0), pl.num_programs(0)
    core = core_ref[0]
    quarter = h_ref.shape[1] // 4

    @pl.when(step == 0)
    def _():
        for at, flip in ((0, 1), (1, 0)):
            for x in (0, 1):
                first = pl.multiple_of((2 * x + (core ^ flip)) * quarter, quarter)
                spot = (2 * at + x) * quarter
                turned[spot : spot + quarter, :] = h_ref[:, pl.ds(first, quarter)].T

    grad = g_ref[...]
    pre = product_nt(grad, down_ref[...]) * slope_ref[...].astype(jnp.float32)
    bias_ref[...] = jnp.sum(pre, 0, keepdims=True)
    pre = pre.astype(jnp.bfloat16)
    add = product_nt(pre, up_ref[...])

    @pl.when(step == 0)
    def _():
        out_ref[...] = add

    @pl.when(step > 0)
    def _():
        out_ref[...] += add

    up = product(turned[...], pre).astype(jnp.bfloat16)
    up_other[...] = up[: 2 * quarter]
    up_mine[...] = up[2 * quarter :]
    down = product_tn(act_ref[...], grad).astype(jnp.bfloat16)

    @pl.when(step < steps // 2)
    def _():
        down_other[...] = down

    @pl.when(step >= steps // 2)
    def _():
        down_mine[...] = down


def ffn_backward(core, grad_ffn, hidden_two, act, slope, w_down, w_up, step=1024):
    rows, width = hidden_two.shape
    units = w_up.shape[1]
    steps = units // step
    inner = steps // 4
    half = steps // 2

    def unit(i, core_ref):
        other = i < half
        j = jnp.where(other, i, i - half)
        c = jnp.where(other, 1 - core_ref[0], core_ref[0])
        return ((j // inner) * 2 + c) * inner + j % inner

    whole = pl.BlockSpec((rows, width), lambda i, core_ref: (0, 0))
    block = pl.BlockSpec((rows, step), lambda i, core_ref: (0, unit(i, core_ref)))
    up_block = pl.BlockSpec((width // 2, step), lambda i, core_ref: (0, unit(i, core_ref)))
    return pl.pallas_call(
        ffn_backward_kernel,
        grid_spec=pltpu.PrefetchScalarGridSpec(
            num_scalar_prefetch=1,
            grid=(steps,),
            in_specs=[
                whole,
                whole,
                block,
                block,
                pl.BlockSpec((step, width), lambda i, core_ref: (unit(i, core_ref), 0)),
                pl.BlockSpec((width, step), lambda i, core_ref: (0, unit(i, core_ref))),
            ],
            out_specs=[
                pl.BlockSpec((step, width), lambda i, core_ref: (jnp.minimum(i, half - 1), 0)),
                pl.BlockSpec((step, width), lambda i, core_ref: (jnp.maximum(i - half, 0), 0)),
                up_block,
                up_block,
                pl.BlockSpec((1, step), lambda i, core_ref: (0, unit(i, core_ref))),
                whole,
            ],
            scratch_shapes=[pltpu.VMEM((width, rows), jnp.bfloat16)],
        ),
        out_shape=[
            jax.ShapeDtypeStruct((units // 2, width), jnp.bfloat16),
            jax.ShapeDtypeStruct((units // 2, width), jnp.bfloat16),
            jax.ShapeDtypeStruct((width // 2, units), jnp.bfloat16),
            jax.ShapeDtypeStruct((width // 2, units), jnp.bfloat16),
            jax.ShapeDtypeStruct((1, units), jnp.float32),
            jax.ShapeDtypeStruct((rows, width), jnp.float32),
        ],
        compiler_params=pltpu.CompilerParams(
            dimension_semantics=("arbitrary",), vmem_limit_bytes=VMEM_LIMIT
        ),
        cost_estimate=pl.CostEstimate(flops=1, bytes_accessed=1, transcendentals=0),
        name="ffn_backward",
    )(core, grad_ffn, hidden_two, act, slope, w_down, w_up)


def half_products_kernel(counts, has_came, core_ref, *refs):
    n_in = 2 * sum(counts) + has_came
    given, out_ref = refs[:n_in], refs[n_in]
    held, out_held, in_sems, out_sems = refs[n_in + 1 : 2 * n_in + 1], *refs[2 * n_in + 1 :]
    coming = [
        pltpu.make_async_copy(source, target, in_sems.at[i])
        for i, (source, target) in enumerate(zip(given, held))
    ]
    if has_came:
        coming[-1].start()
    for copy in coming[: n_in - has_came]:
        copy.start()
    going = []
    at = 0
    for term, count in enumerate(counts):
        total = 0.0
        for pair in range(count):
            for copy in coming[at : at + 2]:
                copy.wait()
            left, right = held[at], held[at + 1]
            at += 2
            quarter = left.shape[1] // 4
            spots = [
                pl.ds(pl.multiple_of((2 * x + core_ref[0]) * quarter, quarter), quarter)
                for x in (0, 1)
            ]
            picked = jnp.concatenate([left[:, spot] for spot in spots], 1)
            total = total + product_tn(picked, right[...])
        if has_came:
            if term == 0:
                coming[-1].wait()
            total = total + held[-1][term].astype(jnp.float32)
        out_held[term] = total.astype(jnp.bfloat16)
        copy = pltpu.make_async_copy(out_held.at[term], out_ref.at[term], out_sems.at[term])
        copy.start()
        going.append(copy)
    for copy in going:
        copy.wait()


def half_products(core, terms, came=None):
    arrays = [matrix for pairs in terms for pair in pairs for matrix in pair]
    shape = (len(terms), arrays[0].shape[1] // 2, arrays[1].shape[1])
    given = arrays if came is None else [*arrays, came]
    return pl.pallas_call(
        functools.partial(
            half_products_kernel, tuple(len(pairs) for pairs in terms), came is not None
        ),
        in_specs=[pl.BlockSpec(memory_space=pltpu.SMEM)]
        + [pl.BlockSpec(memory_space=pl.ANY)] * len(given),
        out_specs=pl.BlockSpec(memory_space=pl.ANY),
        out_shape=jax.ShapeDtypeStruct(shape, jnp.bfloat16),
        scratch_shapes=[pltpu.VMEM(array.shape, jnp.bfloat16) for array in given]
        + [
            pltpu.VMEM(shape, jnp.bfloat16),
            pltpu.SemaphoreType.DMA((len(given),)),
            pltpu.SemaphoreType.DMA((len(terms),)),
        ],
        compiler_params=pltpu.CompilerParams(vmem_limit_bytes=VMEM_LIMIT),
        cost_estimate=pl.CostEstimate(flops=1, bytes_accessed=1, transcendentals=0),
        name="half_products",
    )(core, *given)


def column_sum(matrix):
    return jnp.sum(matrix.astype(jnp.float32), 0)


def layer_norm(residual, gain_vec, shift_vec):
    row_mean = jnp.mean(residual, -1, keepdims=True)
    centred = residual - row_mean
    row_var = jnp.mean(centred * centred, -1, keepdims=True)
    return centred * lax.rsqrt(row_var + 1e-05) * gain_vec + shift_vec


def layer_norm_back(residual, gain_vec, grad):
    row_mean = jnp.mean(residual, -1, keepdims=True)
    centred = residual - row_mean
    row_var = jnp.mean(centred * centred, -1, keepdims=True)
    inverse = lax.rsqrt(row_var + 1e-05)
    xhat = centred * inverse
    dx = grad * gain_vec
    inner = dx - jnp.mean(dx, -1, keepdims=True) - xhat * jnp.mean(dx * xhat, -1, keepdims=True)
    return inner * inverse, jnp.sum(grad * xhat, 0), jnp.sum(grad, 0)


SWAP = ((0, 1), (1, 0))


def swap(value, axis):
    return lax.ppermute(value, axis, SWAP)


class RowSum:
    def __init__(self, part):
        self.part, self.names, self.coming = part, ["y", "z", "w"], None

    def pick(self, flip):
        axis = self.names[0]
        return lax.dynamic_index_in_dim(
            self.part, lax.axis_index(axis) ^ flip, "wzy".index(axis), keepdims=False
        )

    def operands(self):
        part = self.pick(1)
        return [part.reshape(-1, part.shape[-1])]

    def launch(self, operands):
        self.coming = swap(operands[0], self.names[0])

    def add(self):
        part = self.pick(0)
        total = part.astype(jnp.float32) + self.coming.reshape(part.shape).astype(jnp.float32)
        self.names.pop(0)
        self.part = total.astype(jnp.bfloat16) if self.names else total
        self.coming = None

    def finish(self):
        while self.names:
            if self.coming is None:
                self.launch(self.operands())
            self.add()
        return self.part


class WeightSum:
    def __init__(self, other, mine):
        self.other, self.mine = other, mine
        self.names, self.coming = ["c", "xy", "yx", "z", "w"], None

    def operands(self):
        if self.names[0] == "c":
            return [self.other]
        parts = [self.pick(side, 1) for side in range(len(self.sides))]
        return [part.reshape(-1, part.shape[-1]) for part in parts]

    def pick(self, side, flip):
        stage = self.names[0]
        dim = {"xy": (1, 4), "yx": (3, 1), "z": (2,), "w": (1,)}[stage][side]
        here = lax.axis_index(stage[side]) ^ flip
        return lax.dynamic_index_in_dim(self.sides[side], here, dim, keepdims=False)

    def launch(self, operands):
        self.coming = [swap(operand, axis) for operand, axis in zip(operands, self.names[0])]

    def add(self):
        f32, bf16 = jnp.float32, jnp.bfloat16
        stage, coming = self.names[0], self.coming
        if stage == "c":
            total = self.mine(coming[0])
            terms, rows, width = total.shape
            total = total.reshape(terms, 2, 2, 2, 2, rows // 16, width)
            self.sides = [total[..., : width // 2], total[..., width // 2 :]]
        else:
            kept = [self.pick(side, 0) for side in range(len(coming))]
            self.sides = [
                part.astype(f32) + came.reshape(part.shape).astype(f32)
                for part, came in zip(kept, coming)
            ]
            if stage != "w":
                self.sides = [side.astype(bf16) for side in self.sides]
            if stage == "yx":
                self.sides = [jnp.concatenate(self.sides, -1)]
        self.names.pop(0)
        self.coming = None

    def finish(self):
        while self.names:
            if self.coming is None:
                self.launch(self.operands())
            self.add()
        return self.sides[0]


class Whole:
    def __init__(self, axes, parts):
        self.names, self.coming = [], None
        self.parts = [
            lax.psum_scatter(part.astype(jnp.bfloat16), axes, scatter_dimension=0, tiled=True)
            for part in parts
        ]

    def finish(self):
        return jnp.stack(self.parts).astype(jnp.float32)


def begin(value, *transfers):
    live = [t for t in transfers if t.names]
    if not live:
        return value
    value, operands = lax.optimization_barrier((value, [t.operands() for t in live]))
    for t, ready in zip(live, operands):
        t.launch(ready)
    return value


def advance(value, *transfers):
    live = [t for t in transfers if t.coming is not None]
    if not live:
        return value
    value, arrived = lax.optimization_barrier((value, [t.coming for t in live]))
    for t, coming in zip(live, arrived):
        t.coming = coming
        t.add()
    return begin(value, *live)


class Rows:
    def __init__(self, part):
        self.part, self.names, self.coming = part, (), None

    def finish(self):
        return self.part.astype(jnp.float32)


class Known:
    def __init__(self, parts):
        self.parts, self.names, self.coming = parts, (), None

    def finish(self, place):
        return self.parts


class RowGathering:
    def __init__(self, block, cuts):
        self.block, self.cuts, self.names = block, cuts, ["w", "z", "y"]
        self.coming = None

    def operands(self):
        return [self.block]

    def launch(self, operands):
        (self.block,) = operands
        self.coming = swap(self.block, self.names[0])

    def add(self):
        self.names.pop(0)
        self.block = jnp.stack([self.block, self.coming])
        self.coming = None

    def finish(self, place):
        while self.names:
            if self.coming is None:
                self.launch(self.operands())
            self.add()
        return assemble_rows(place, self.cuts, self.block)


def put_blocks(own, source, spans, outs, lead):
    shard = source.shape[-2]
    for y, z, w in itertools.product(range(2), range(2), range(2)):
        place = ((own[0] ^ w) * 2 + (own[1] ^ z)) * 2 + (own[2] ^ y)
        rows = pl.ds(pl.multiple_of(place * shard, shard), shard)
        for first, out, column, count in spans:
            outs[out][rows, column : column + count] = source[
                (*lead(y), z, w, slice(None), slice(first, first + count))
            ]


def assemble_kernel(spans, place_ref, left_own, right_own, left_came, right_came, *outs):
    own = (place_ref[2], place_ref[3], place_ref[4])
    core = pl.program_id(0)
    for which, left, right in ((0, left_own, right_own), (1, left_came, right_came)):

        @pl.when(core == which)
        def _(left=left, right=right):
            put_blocks(own, left, spans[0], outs, lambda y: (0, y))
            put_blocks(own, right, spans[1], outs, lambda y: (y, 0))


def assemble(place, spans, arrays, shapes):
    left_own, right_own, _, _ = arrays
    shard = left_own.shape[-2]

    def left_spec(which):
        def at(core, x, _):
            return (jnp.where(core == which, x, 1 - which), 0, 0, 0, 0, 0)

        return pl.BlockSpec((1, 2, 2, 2, shard, left_own.shape[-1]), at)

    def right_spec(which):
        def at(core, x, _):
            return (0, jnp.where(core == which, x, 1 - which), 0, 0, 0, 0)

        return pl.BlockSpec((2, 1, 2, 2, shard, right_own.shape[-1]), at)

    def out_at(core, x, place_ref):
        return ((place_ref[0] ^ x) * 2 + (place_ref[1] ^ core), 0)

    return pl.pallas_call(
        functools.partial(assemble_kernel, spans),
        grid_spec=pltpu.PrefetchScalarGridSpec(
            num_scalar_prefetch=1,
            grid=(2, 2),
            in_specs=[left_spec(0), right_spec(0), left_spec(1), right_spec(1)],
            out_specs=[pl.BlockSpec((8 * shard, shape[1]), out_at) for shape in shapes],
        ),
        out_shape=[jax.ShapeDtypeStruct(shape, jnp.bfloat16) for shape in shapes],
        compiler_params=pltpu.CompilerParams(
            dimension_semantics=("arbitrary", "arbitrary"), vmem_limit_bytes=VMEM_LIMIT
        ),
        cost_estimate=pl.CostEstimate(
            flops=0, transcendentals=0, bytes_accessed=sum(4 * array.size for array in arrays)
        ),
        name="assemble",
    )(place, *arrays)


def assemble_rows_kernel(cuts, place_ref, source, *outs):
    own = (place_ref[2], place_ref[3], place_ref[4])
    for out, (first, count) in zip(outs, cuts):
        for y, z, w in itertools.product(range(2), range(2), range(2)):
            block = ((own[0] ^ w) * 2 + (own[1] ^ z)) * 2 + (own[2] ^ y)
            rows = pl.ds(pl.multiple_of(block * count, count), count)
            out[rows, :] = source[y, z, w, first : first + count, :]


def assemble_rows(place, cuts, gathered):
    width = gathered.shape[-1]
    return pl.pallas_call(
        functools.partial(assemble_rows_kernel, cuts),
        in_specs=[pl.BlockSpec(memory_space=pltpu.SMEM), pl.BlockSpec(memory_space=pltpu.VMEM)],
        out_specs=[pl.BlockSpec(memory_space=pltpu.VMEM) for _ in cuts],
        out_shape=[jax.ShapeDtypeStruct((8 * count, width), jnp.bfloat16) for _, count in cuts],
        compiler_params=pltpu.CompilerParams(vmem_limit_bytes=VMEM_LIMIT),
        cost_estimate=pl.CostEstimate(
            flops=0, transcendentals=0, bytes_accessed=4 * gathered.size
        ),
        name="assemble_rows",
    )(place, gathered)


class Gathering:
    def __init__(self, block, cut, spans, shapes):
        self.sides, self.cut = [block], cut
        self.spans, self.shapes = spans, shapes
        self.names, self.coming = ["w", "z", "yx", "xy", "cc"], None

    def operands(self):
        return self.sides

    def launch(self, operands):
        self.sides = operands
        self.coming = [swap(side, axis) for side, axis in zip(operands, self.names[0])]

    def add(self):
        stage = self.names.pop(0)
        coming, self.coming = self.coming, None
        if stage == "cc":
            self.arrived = coming
        elif stage == "z":
            pair = [self.sides[0], coming[0]]
            self.sides = [
                jnp.stack([block[..., : self.cut] for block in pair]),
                jnp.stack([block[..., self.cut :] for block in pair]),
            ]
        else:
            self.sides = [jnp.stack(pair) for pair in zip(self.sides, coming)]

    def finish(self, place):
        while self.names:
            if self.coming is None:
                self.launch(self.operands())
            self.add()
        return assemble(place, self.spans, [*self.sides, *self.arrived], self.shapes)


class Links:
    def __init__(self, mesh):
        self.fast = dict(mesh.shape) == {"fsdp": 4, "ctx": 8}
        if self.fast:
            self.mesh = Mesh(mesh.devices.reshape(2, 2, 2, 2, 2), ("x", "c", "w", "z", "y"))
            self.rows, self.ctx = ("x", "c"), ("w", "z", "y")
        else:
            self.mesh, self.rows, self.ctx = mesh, ("fsdp",), ("ctx",)
        self.every = self.rows + self.ctx

    def place(self):
        axes = self.every if self.fast else ()
        return jnp.stack([lax.axis_index(axis).astype(jnp.int32) for axis in axes or self.rows])

    def gather(self, weights, cut):
        if not self.fast:
            return Known([lax.all_gather(w, self.every, axis=0, tiled=True) for w in weights])
        shapes = tuple((32 * w.shape[0], w.shape[1]) for w in weights)
        block = weights[0] if len(weights) == 1 else jnp.concatenate(weights, 1)
        first, left, right = 0, [], []
        for out, weight in enumerate(weights):
            count = weight.shape[1]
            low = min(max(cut - first, 0), count)
            if low:
                left.append((first, out, 0, low))
            if low < count:
                right.append((first + low - cut, out, low, count - low))
            first += count
        return Gathering(block, cut, (tuple(left), tuple(right)), shapes)

    def gather_once(self, weights):
        return lax.all_gather(jnp.concatenate(weights, 1), self.every, axis=0, tiled=True)

    def gather_rows(self, parts):
        if not self.fast:
            return Known([lax.all_gather(part, self.ctx, axis=0, tiled=True) for part in parts])
        cuts, first = [], 0
        for part in parts:
            cuts.append((first, part.shape[0]))
            first += part.shape[0]
        return RowGathering(jnp.concatenate(parts, 0), tuple(cuts))

    def weight_sum(self, terms):
        if not self.fast:
            return Whole(
                self.every,
                [sum(product_tn(left, right) for left, right in pairs) for pairs in terms],
            )
        core = lax.axis_index("c").astype(jnp.int32).reshape(1)
        return WeightSum(
            half_products(1 - core, terms), lambda came: half_products(core, terms, came)
        )

    def row_sum(self, part):
        part = part.astype(jnp.bfloat16)
        if not self.fast:
            return Rows(lax.psum_scatter(part, self.ctx, scatter_dimension=0, tiled=True))
        return RowSum(part.reshape(2, 2, 2, part.shape[0] // 8, part.shape[1]))


def body(
    links,
    prompt_in,
    cont_in,
    encoder,
    prompt_start,
    cont_start,
    self_proj,
    self_out,
    cross_query,
    cross_kv,
    cross_out,
    up_proj,
    down_proj,
    vec_bias,
    up_bias,
    ln_gain,
    ln_bias,
    prompt_cot,
    cont_cot,
):
    f32, bf16 = jnp.float32, jnp.bfloat16
    shard, width = self_out.shape
    prompt_rows, slot_len = prompt_in.shape[1], cont_in.shape[2]
    block_index = lax.axis_index(links.ctx)
    ctx_count = lax.axis_size(links.ctx)
    prompt_len = prompt_rows * ctx_count
    enc_rows = encoder.shape[1]
    hidden = up_bias.shape[0] // shard
    scale = HDIM ** (-0.5)

    small = jnp.concatenate(
        [vec_bias.T, ln_gain.T, ln_bias.T, up_bias.reshape(hidden, shard).T], 1
    )
    small = jnp.pad(small, ((0, 0), (0, 128 - small.shape[1])))
    place = links.place()
    rows_in = links.gather_rows([prompt_in[0], encoder[0]])
    first = links.gather([self_proj, small], 13 * 128)
    second = links.gather([self_out, cross_query, cross_kv, cross_out], 20 * 128)
    up = links.gather([up_proj], 16 * 128)
    tokens = jnp.concatenate([prompt_in[0], cont_in[0, 0]], 0)
    tokens = begin(tokens, first, rows_in)
    tokens = advance(tokens, first)
    tokens = advance(tokens, rows_in)
    tokens = advance(tokens, first)
    tokens = begin(tokens, second)
    tokens = advance(tokens, first)
    tokens = advance(tokens, rows_in, second)
    tokens = advance(tokens, first)
    tokens = begin(tokens, up)
    tokens = advance(tokens, first)
    self_w, small = first.finish(place)
    w_q, w_kv = self_w[:, :width], self_w[:, width:]
    small = small.astype(f32).T
    biases, gains, shifts = small[:7], small[7:10], small[10:13]
    hidden_bias = (
        small[13 : 13 + hidden]
        .reshape(hidden, width // shard, shard)
        .transpose(1, 0, 2)
        .reshape(hidden * width)
    )

    every_begin = cont_start[0]
    own_begin = lax.dynamic_index_in_dim(every_begin, block_index, 0, keepdims=False)
    scalars = jnp.stack([prompt_start[0], own_begin, block_index.astype(jnp.int32)])
    cont_rows = tokens[prompt_rows:]
    row_total = tokens.shape[0]
    row_spot = jnp.arange(row_total, dtype=jnp.int32)
    valid_rows = jnp.where(
        row_spot < prompt_rows,
        block_index * prompt_rows + row_spot >= prompt_start[0],
        row_spot - prompt_rows >= own_begin,
    ).astype(f32)[:, None]
    valid_count = (prompt_len - prompt_start[0] + jnp.sum(slot_len - every_begin)).astype(f32)

    kv_bias = jnp.concatenate([jnp.zeros((width,), f32), biases[1]])
    queries = ((product(tokens, w_q) + biases[0]) * scale).astype(bf16)
    cont_kv = (product(cont_rows, w_kv) + kv_bias).astype(bf16)
    (queries, cont_kv) = advance((queries, cont_kv), second, up)
    queries = advance(queries, rows_in)
    prompt_all, enc_all = rows_in.finish(place)
    prompt_kv = (product(prompt_all, w_kv) + kv_bias).astype(bf16)
    plan = self_plan(prompt_rows, prompt_len, slot_len)
    prompt_kv, down_proj = advance((prompt_kv, down_proj), second, up)
    w_down = lax.all_gather(down_proj, links.every, axis=0, tiled=True)
    attn, self_log = attend_forward(scalars, queries, [prompt_kv, cont_kv], plan, prompt_rows)
    attn = advance(attn, second)
    attn = advance(attn, second, up)
    w_so, w_cq, w_ckv, w_co = second.finish(place)
    branch_self = product(attn, w_so) + biases[2]
    resid_one = tokens.astype(f32) + branch_self
    hidden_one = layer_norm(resid_one, gains[0], shifts[0]).astype(bf16)

    enc_bias = jnp.concatenate([jnp.zeros((width,), f32), biases[4]])
    enc_kv = (product(enc_all, w_ckv) + enc_bias).astype(bf16)
    cross_queries = ((product(hidden_one, w_cq) + biases[3]) * scale).astype(bf16)
    enc_len = enc_all.shape[0]
    cross_attn, cross_log = attend_forward(
        None, cross_queries, [enc_kv], cross_plan(row_total, enc_len, 320), 0
    )
    cross_attn = advance(cross_attn, up)
    branch_cross = product(cross_attn, w_co) + biases[5]
    resid_two = hidden_one.astype(f32) + branch_cross
    hidden_two = layer_norm(resid_two, gains[1], shifts[1]).astype(bf16)
    hidden_two = advance(hidden_two, up)
    (w_up,) = up.finish(place)

    act, slope, branch_ffn = ffn_forward(hidden_two, w_up, hidden_bias, w_down)
    branch_ffn = branch_ffn + biases[6]
    resid_three = hidden_two.astype(f32) + branch_ffn
    output = layer_norm(resid_three, gains[2], shifts[2]).astype(bf16)

    members = (tokens, branch_self, hidden_one, branch_cross, hidden_two, branch_ffn)
    squares = jnp.stack(
        [jnp.sum(valid_rows * jnp.square(member.astype(f32)), 0) for member in members]
    )
    grad_out = jnp.concatenate([prompt_cot[0], cont_cot[0, 0]], 0).astype(f32)
    grad_three, gain_three, shift_three = layer_norm_back(resid_three, gains[2], grad_out)
    grad_ffn = grad_three.astype(bf16)
    half_width = width // 2
    if links.fast:
        core = lax.axis_index("c").astype(jnp.int32).reshape(1)
        down_other, down_mine, up_other, up_mine, up_bias_part, back_ffn = ffn_backward(
            core, grad_ffn, hidden_two, act, slope, w_down, w_up
        )

        def add_to(mine):
            return lambda came: (mine.astype(f32) + came[0].astype(f32)).astype(bf16)[None]

        down_sum = WeightSum(down_other[None], add_to(down_mine))
        up_sum = WeightSum(up_other[None], add_to(up_mine))
    else:
        grad_pre = (product_nt(grad_ffn, w_down) * slope.astype(f32)).astype(bf16)
        down_sum = links.weight_sum([[(act, grad_ffn)]])
        up_sum = links.weight_sum([[(hidden_two, grad_pre)]])
        up_bias_part = column_sum(grad_pre)
        back_ffn = product_nt(grad_pre, w_up)
    back_ffn = begin(back_ffn, down_sum, up_sum)
    grad_hidden_two = grad_three + back_ffn
    grad_two, gain_two, shift_two = layer_norm_back(resid_two, gains[1], grad_hidden_two)
    grad_cross = grad_two.astype(bf16)
    grad_cattn = product_nt(grad_cross, w_co).astype(bf16)
    grad_cattn = advance(grad_cattn, down_sum, up_sum)
    cross_gq, cross_gk, cross_gv = attend_backward(
        None,
        cross_queries,
        grad_cattn,
        cross_attn,
        cross_log,
        [enc_kv],
        cross_plan(row_total, enc_len, 384),
        0,
        512,
        (0,),
    )
    grad_cq = (cross_gq.astype(f32) * scale).astype(bf16)
    enc_back = product_nt(cross_gk[0], w_ckv[:, :width]) + product_nt(
        cross_gv[0], w_ckv[:, width:]
    )
    enc_sum = links.row_sum(enc_back)
    grad_hidden_one = grad_two + product_nt(grad_cq, w_cq)
    grad_one, gain_one, shift_one = layer_norm_back(resid_one, gains[0], grad_hidden_one)
    grad_self = grad_one.astype(bf16)
    mid_sum = links.weight_sum(
        [
            [(cross_attn, grad_cross)],
            [(hidden_one, grad_cq)],
            [(attn, grad_self)],
            [(enc_all, cross_gk[0])],
            [(enc_all, cross_gv[0])],
        ]
    )
    if links.fast:
        grad_self, mid_sum.other = advance((grad_self, mid_sum.other), down_sum, up_sum)
    grad_self = begin(grad_self, mid_sum)
    grad_attn = product_nt(grad_self, w_so).astype(bf16)
    small_part = jnp.concatenate(
        [
            squares,
            jnp.stack(
                [
                    column_sum(grad_self),
                    column_sum(grad_cq),
                    column_sum(cross_gv[0]),
                    column_sum(grad_cross),
                    column_sum(grad_ffn),
                    gain_one,
                    gain_two,
                    gain_three,
                    shift_one,
                    shift_two,
                    shift_three,
                ]
            ),
            up_bias_part.reshape(width // shard, hidden, shard)
            .transpose(1, 0, 2)
            .reshape(hidden, width),
        ],
        0,
    )
    grad_attn, small_part = lax.optimization_barrier((grad_attn, small_part))
    grad_attn = advance(grad_attn, mid_sum, down_sum, up_sum)
    self_args = (queries, grad_attn, attn, self_log, [prompt_kv, cont_kv], plan, prompt_rows)
    part_gq, prompt_gk, prompt_gv = attend_backward(scalars, *self_args, 1024, (0,))
    prompt_gk, prompt_gv = prompt_gk[0], prompt_gv[0]
    w_k, w_v = w_kv[:, :width], w_kv[:, width:]
    part_gq = advance(part_gq, up_sum, mid_sum, down_sum)
    prompt_sum = links.row_sum(product_nt(prompt_gk, w_k) + product_nt(prompt_gv, w_v))
    part_gq = begin(part_gq, prompt_sum)
    part_gq = advance(part_gq, down_sum, up_sum)
    self_gq, cont_gk, cont_gv = attend_backward(scalars, *self_args, 512, (1,), part_gq)
    cont_gk, cont_gv = cont_gk[0], cont_gv[0]
    self_gq = advance(self_gq, mid_sum, prompt_sum)
    self_gq = begin(self_gq, enc_sum)
    grad_q = (self_gq.astype(f32) * scale).astype(bf16)

    last_part = jnp.stack([column_sum(grad_q), column_sum(prompt_gv) + column_sum(cont_gv)])
    small_part = jnp.concatenate(
        [small_part, last_part, jnp.zeros((32 - small_part.shape[0] - 2, width), f32)], 0
    )
    small_all = lax.all_gather(small_part, links.every, axis=0, tiled=True)
    self_sum = links.weight_sum(
        [
            [(tokens, grad_q)],
            [(prompt_all, prompt_gk), (cont_rows, cont_gk)],
            [(prompt_all, prompt_gv), (cont_rows, cont_gv)],
        ]
    )
    input_grad = grad_one + product_nt(grad_q, w_q)
    cont_grad = input_grad[prompt_rows:] + product_nt(cont_gk, w_k) + product_nt(cont_gv, w_v)
    if links.fast:
        cont_grad, self_sum.other = advance(
            (cont_grad, self_sum.other), mid_sum, prompt_sum, enc_sum
        )
    cont_grad = begin(cont_grad, self_sum)
    cont_grad = advance(cont_grad, self_sum)
    cont_grad = advance(cont_grad, self_sum, mid_sum, prompt_sum, enc_sum)
    cont_grad = advance(cont_grad, self_sum)
    cont_grad = advance(cont_grad, self_sum, enc_sum)
    cont_grad = cont_grad[None, None]
    prompt_grad = (input_grad[:prompt_rows] + prompt_sum.finish())[None]
    encoder_grad = enc_sum.finish()[None]
    up_total, down_total = up_sum.finish()[0], down_sum.finish()[0]
    co_total, cq_total, so_total, ck_total, cv_total = mid_sum.finish()
    ckv_total = jnp.concatenate([ck_total, cv_total], 1)
    sin_total = jnp.concatenate([*self_sum.finish()], 1)
    small_all = small_all.reshape(-1, ctx_count, 32, width)
    group = lax.axis_index(links.rows)
    squares = jnp.sum(lax.dynamic_index_in_dim(small_all, group, 0, keepdims=False)[:, :6], (0, 2))
    statistics = (squares / (valid_count * width))[None]
    at = lax.axis_index(links.every) * shard
    sums = jnp.sum(lax.dynamic_slice_in_dim(small_all, at, shard, 3), (0, 1))
    bias_total = jnp.concatenate([sums[21:23], sums[6:11]])
    gain_total, shift_total = sums[11:14], sums[14:17]
    up_bias_total = sums[17 : 17 + hidden].reshape(hidden * shard)
    return (
        output[:prompt_rows][None],
        output[prompt_rows:][None, None],
        prompt_grad,
        cont_grad,
        encoder_grad,
        sin_total,
        so_total,
        cq_total,
        ckv_total,
        co_total,
        up_total,
        down_total,
        bias_total,
        up_bias_total,
        gain_total,
        shift_total,
        statistics,
    )


def solution(mesh):
    links = Links(mesh)
    fs, ctx, every = links.rows, links.ctx, links.every
    group = P(fs, ctx, None)
    slots = P(fs, ctx, None, None)
    weight = P(every, None)
    vectors = P(None, every)
    return jax.shard_map(
        functools.partial(body, links),
        mesh=links.mesh,
        in_specs=(group, slots, group, P(fs), P(fs, None))
        + (weight,) * 7
        + (vectors, P(every), vectors, vectors, group, slots),
        out_specs=(group, slots, group, slots, group)
        + (weight,) * 7
        + (vectors, P(every), vectors, vectors, P(fs, None)),
        check_vma=False,
    )
```
